32 devices in a mesh: section: 2 (over core), seq: 4 (over y, x), dp: 4 (over z).
Axes of the slice: x: 2, y: 2, z: 4, core: 2. Of those that a mesh axis runs over, the one named last changes fastest.
Arguments:
- section_input: bfloat16 [2, 4, 512, 4096], P('section', 'dp', 'seq'), may hold values from -6 to 6
- saved_qkv: bfloat16 [2, 4, 512, 3, 2048], P('section', 'dp', None, None, 'seq'), may hold values from -14 to 14
- modulation: float32 [2, 4, 2, 4096], P('section', 'dp'), may hold values from -4 to 4
- w_qkv: bfloat16 [2, 4096, 3, 2048], P('section', 'dp', None, 'seq'), may hold values from -0.09375 to 0.09375
- w_out: bfloat16 [2, 2048, 4096], P('section', 'seq'), may hold values from -0.125 to 0.125
- lengths: int32 [4], P('dp'), may hold values from 1 to 512, 1280 in all
- student_out: bfloat16 [4, 512, 4096], P('dp', 'seq'), may hold values from -6 to 6
- teacher_target: bfloat16 [4, 512, 4096], P('dp', 'seq'), may hold values from -6 to 6
Outputs:
- grad_input: bfloat16 [2, 4, 512, 4096], P('section', 'dp', 'seq')
- grad_out: bfloat16 [2, 2048, 4096], P('section', 'seq', 'dp')
The draws below stay inside these ranges and needn't reach their ends.
Inputs may be any that keep to these rules, and one draw needn't show every extreme that they name: `lengths`: at least one micro-batch is 512 tokens long.
All inputs are finite; a program needn't handle non-finite values. No bound on the sum of `lengths` on one device may be relied on, other than what follows from the above.
Results may differ from the reference program's by a relative error of at most 0.014.
Values may be sent and summed in bfloat16 or wider, within the bound.
No kernel may reach another device: no remote copies, remote signals or barrier semaphores. Data moves between devices by JAX's collectives and lax.ppermute only.
A program may use at most 192 MiB of HBM per device.

```python
import math
import jax
import jax.numpy as jnp
import numpy as np
from jax import lax

D = 4096
HEAD_DIM = 128
HW = 2048
CAP = 512
SECTIONS = 2
BATCH = 4


def draw_saved_qkv(key, part):
    key_main = jax.random.fold_in(key, 11)
    full_shape = (SECTIONS, BATCH, CAP, 3, HW)
    values = jnp.clip(jax.random.normal(key_main, full_shape, jnp.float32), -5.0, 5.0)
    return values.astype(jnp.bfloat16)


def block_levels(stream_key, shape, cuts, least, largest):
    gain = 1.0
    for axis_at, blocks in cuts:
        heights = jax.random.uniform(jax.random.fold_in(jax.random.fold_in(stream_key, 6), axis_at), (blocks,), jnp.float32, least / len(cuts), largest / len(cuts))
        gain = gain * jnp.repeat(jnp.exp(heights), shape[axis_at] // blocks).reshape((-1,) + (1,) * (len(shape) - 1 - axis_at))
    return gain


def profile(count, total, bound, skew):
    weights = [(1 << 20) // math.isqrt(standing ** skew) + 1 for standing in range(2, count + 1)]
    surplus, given = total - bound - (count - 1), [1] * (count - 1)
    while surplus > 0:
        movable = [i for i in range(count - 1) if given[i] < bound]
        whole, budget = sum([weights[i] for i in movable]), surplus
        for i in movable:
            addition = min(bound - given[i], max(1, budget * weights[i] // whole), surplus)
            given[i] = given[i] + addition
            surplus = surplus - addition
    return np.array([bound] + given)


def ragged_sizes(rng, number_of, total, reach, slope):
    if number_of == 2:
        one = jax.random.randint(rng, (), max(1, total - reach), min(reach, total - 1) + 1)
        return jnp.stack([one, total - one])
    sizes = jnp.asarray(profile(number_of, total, reach, slope), jnp.int32)
    pairs = (number_of - 1) // 2
    giver, sink = sizes[1:1 + 2 * pairs:2], sizes[2:2 + 2 * pairs:2]
    room = jnp.minimum(giver - 1, reach - sink)
    shifted = jax.random.randint(jax.random.fold_in(rng, 1), (pairs,), 0, 1 << 20) % (room + 1)
    sizes = sizes.at[1:1 + 2 * pairs:2].set(giver - shifted).at[2:2 + 2 * pairs:2].set(sink + shifted)
    return sizes[jax.random.permutation(jax.random.fold_in(rng, 2), number_of)]


def centred(stream_key, dims, width, most, split=(), kind=jnp.bfloat16):
    factor_of = block_levels(stream_key, dims, split, -0.22, 0.18) if split else 1.0
    drawn = jax.random.normal(stream_key, dims, jnp.float32) * width * factor_of
    return jnp.minimum(jnp.maximum(drawn, -most), most).astype(kind)


def setup_inputs(seed: int = 0) -> dict:
    key_of = jax.random.split(jax.random.key(seed), 9)
    return {
        "section_input": centred(key_of[0], (SECTIONS, BATCH, CAP, D), 1.0, 6.0, ((0, 2), (1, 4), (2, 4))),
        "saved_qkv": draw_saved_qkv(jax.random.fold_in(key_of[8], 71), 0),
        "modulation": centred(key_of[2], (SECTIONS, BATCH, 2, D), 0.7, 4.0, ((0, 2), (1, 4)), jnp.float32),
        "w_qkv": centred(key_of[3], (SECTIONS, D, 3, HW), D ** -0.5, 0.09375, ((0, 2), (1, 4), (3, 4))),
        "w_out": centred(key_of[4], (SECTIONS, HW, D), HW ** -0.5, 0.125, ((0, 2), (1, 4))),
        "lengths": ragged_sizes(key_of[5], BATCH, BATCH * CAP * 5 // 8, CAP, 1).astype(jnp.int32),
        "student_out": centred(key_of[6], (BATCH, CAP, D), 1.0, 6.0, ((0, 4), (1, 4))),
        "teacher_target": centred(key_of[7], (BATCH, CAP, D), 1.0, 6.0, ((0, 4), (1, 4))),
    }


def widen(tensor):
    return lax.optimization_barrier(tensor).astype(jnp.float32)

def layer_norm_parts(tokens):
    values = tokens.astype(jnp.float32)
    center = values - lax.optimization_barrier(jnp.mean(values, axis=-1, keepdims=True))
    variance = lax.optimization_barrier(jnp.mean(center * center, axis=-1, keepdims=True))
    inverse = lax.rsqrt(variance + 1e-06)
    return (center * inverse, inverse)

def attend_backward(saved_rows, d_attn, live_keys, head_size):
    row_total = saved_rows.shape[0]
    feature_width = saved_rows.shape[2]
    head_count = feature_width // head_size
    queries = saved_rows[:, 0].reshape(row_total, head_count, head_size).astype(jnp.float32)
    key_rows = saved_rows[:, 1].reshape(row_total, head_count, head_size).astype(jnp.float32)
    value_rows = saved_rows[:, 2].reshape(row_total, head_count, head_size).astype(jnp.float32)
    factor = 1.0 / math.sqrt(head_size)
    scores = jnp.einsum('qhd,khd->hqk', queries, key_rows) * factor
    scores = jnp.where(live_keys[None, None, :], scores, -1e+30)
    peak_score = lax.optimization_barrier(jnp.max(scores, axis=-1, keepdims=True))
    weights = jnp.exp(scores - peak_score)
    weights = weights / lax.optimization_barrier(jnp.sum(weights, axis=-1, keepdims=True))
    rounded = widen(weights.astype(jnp.bfloat16))
    attn_mixed = jnp.einsum('hqk,khd->qhd', rounded, value_rows).astype(jnp.bfloat16)
    upstream = d_attn.reshape(row_total, head_count, head_size).astype(jnp.float32)
    d_weights = jnp.einsum('qhd,khd->hqk', upstream, value_rows)
    delta_rows = jnp.einsum('qhd,qhd->hq', upstream, widen(attn_mixed))
    d_scores = widen((weights * (d_weights - delta_rows[:, :, None]) * factor).astype(jnp.bfloat16))
    grad_q = jnp.einsum('hqk,khd->qhd', d_scores, key_rows).astype(jnp.bfloat16)
    grad_k = jnp.einsum('hqk,qhd->khd', d_scores, queries).astype(jnp.bfloat16)
    grad_v = jnp.einsum('hqk,qhd->khd', rounded, upstream).astype(jnp.bfloat16)
    stacked = jnp.stack([grad_q, grad_k, grad_v], axis=1).reshape(row_total, 3, feature_width)
    return (attn_mixed.reshape(row_total, feature_width), stacked)

def reference(section_input, saved_qkv, modulation, w_qkv, w_out, lengths, student_out, teacher_target):
    section_total = section_input.shape[0]
    batch_total = section_input.shape[1]
    capacity = section_input.shape[2]
    model_width = section_input.shape[3]
    attn_width = saved_qkv.shape[4]
    key_positions = jnp.arange(capacity, dtype=jnp.int32)
    grad_rows = [[None] * batch_total for section_pos in range(section_total)]
    out_grads = [jnp.zeros((attn_width, model_width), jnp.float32) for section_pos in range(section_total)]
    for batch_row in range(batch_total):
        live_keys = key_positions < lengths[batch_row]
        gap = student_out[batch_row].astype(jnp.float32) - teacher_target[batch_row].astype(jnp.float32)
        d_output = jnp.where(live_keys[:, None], gap, 0.0).astype(jnp.bfloat16)
        for section_pos in reversed(range(section_total)):
            normed, inverse = layer_norm_parts(section_input[section_pos, batch_row])
            scale_term = modulation[section_pos, batch_row, 0]
            gate_term = modulation[section_pos, batch_row, 1]
            d_branch = (gate_term * d_output.astype(jnp.float32)).astype(jnp.bfloat16)
            d_attn = jnp.dot(d_branch, w_out[section_pos].T, preferred_element_type=jnp.float32).astype(jnp.bfloat16)
            attn_mixed, d_saved = attend_backward(saved_qkv[section_pos, batch_row], d_attn, live_keys, HEAD_DIM)
            flat_grads = d_saved.reshape(capacity, 3 * attn_width)
            weight_flat = w_qkv[section_pos].reshape(model_width, 3 * attn_width)
            d_mod = jnp.dot(flat_grads, weight_flat.T, preferred_element_type=jnp.float32)
            d_norm = d_mod * (1.0 + scale_term)
            d_layer = inverse * (d_norm - lax.optimization_barrier(jnp.mean(d_norm, axis=-1, keepdims=True)) - normed * lax.optimization_barrier(jnp.mean(d_norm * normed, axis=-1, keepdims=True)))
            d_input = (d_output.astype(jnp.float32) + d_layer).astype(jnp.bfloat16)
            out_grads[section_pos] = out_grads[section_pos] + jnp.dot(attn_mixed.T, d_branch, preferred_element_type=jnp.float32)
            grad_rows[section_pos][batch_row] = d_input
            d_output = d_input
    grad_input = jnp.stack([jnp.stack(grad_rows[section_pos], axis=0) for section_pos in range(section_total)], axis=0)
    grad_out = jnp.stack(out_grads, axis=0).astype(jnp.bfloat16)
    return (grad_input, grad_out)
```

```python
import functools
import math

import jax
import jax.numpy as jnp
from jax import lax
from jax.experimental import pallas as pl
from jax.experimental.pallas import tpu as pltpu
from jax.sharding import PartitionSpec as P

HEAD_DIM = 128
AXES = ("section", "seq", "dp")
F32 = jnp.float32
BF16 = jnp.bfloat16


def dot_nt(left, right):
    return lax.dot_general(left, right, (((1,), (1,)), ((), ())), preferred_element_type=F32)


def dot_nn(left, right):
    return lax.dot_general(left, right, (((1,), (0,)), ((), ())), preferred_element_type=F32)


def dot_tn(left, right):
    return lax.dot_general(left, right, (((0,), (0,)), ((), ())), preferred_element_type=F32)


def d_attn_kernel(info, *refs):
    blocks, w_out, out = refs[:-2], refs[-2], refs[-1]
    rows = blocks[0].shape[0]
    me = info[0]
    for r, block in enumerate(blocks):
        start = pl.multiple_of((me ^ r) * rows, rows)
        out[pl.ds(start, rows), :] = dot_nt(block[...], w_out[...]).astype(BF16)


def d_attn_call(info, blocks, w_out):
    rows, width = blocks[0].shape
    heads_width = w_out.shape[0]
    whole = lambda shape: pl.BlockSpec(shape, lambda step, info: (0, 0))
    count = len(blocks)
    return pl.pallas_call(
        d_attn_kernel,
        out_shape=jax.ShapeDtypeStruct((rows * count, heads_width), BF16),
        grid_spec=pltpu.PrefetchScalarGridSpec(
            num_scalar_prefetch=1,
            grid=(1,),
            in_specs=[whole((rows, width))] * count + [whole(w_out.shape)],
            out_specs=whole((rows * count, heads_width)),
        ),
        compiler_params=pltpu.CompilerParams(vmem_limit_bytes=40 * 1024 * 1024),
        cost_estimate=pl.CostEstimate(
            flops=2 * rows * count * heads_width * width,
            bytes_accessed=2 * (rows * count * width + heads_width * width),
            transcendentals=0,
        ),
    )(info, *blocks, w_out)


def attend_kernel(slot, info, saved, d_attn, weight, attn_rel, *rest):
    outs, (grads, attn_all, partial, w_vmem, w_sem) = rest[:-5], rest[-5:]
    count = len(outs)
    rows = outs[0].shape[0]
    capacity = d_attn.shape[0]
    head = pl.program_id(0)
    head_count = pl.num_programs(0)
    me, live = info[0], info[2 + slot]
    factor = 1.0 / math.sqrt(HEAD_DIM)
    w_copy = pltpu.make_async_copy(weight, w_vmem, w_sem)

    @pl.when(head == 0)
    def _():
        w_copy.start()

    columns = pl.ds(pl.multiple_of(head * HEAD_DIM, HEAD_DIM), HEAD_DIM)

    def one_head(size):
        queries, keys, values = saved[0, :size], saved[1, :size], saved[2, :size]
        upstream = d_attn[:size]
        scores = dot_nt(queries, keys) * factor
        alive = lax.broadcasted_iota(jnp.int32, (1, size), 1) < live
        scores = jnp.where(alive, scores, -1e30)
        weights = jnp.exp(scores - jnp.max(scores, axis=1, keepdims=True))
        weights = weights / jnp.sum(weights, axis=1, keepdims=True)
        rounded = weights.astype(BF16)
        mixed = dot_nn(rounded, values).astype(BF16)
        attn_all[:size, columns] = mixed
        delta = jnp.sum(upstream.astype(F32) * mixed.astype(F32), axis=1, keepdims=True)
        d_scores = (weights * (dot_nt(upstream, values) - delta) * factor).astype(BF16)
        grads[0, :size, columns] = dot_nn(d_scores, keys).astype(BF16)
        grads[1, :size, columns] = dot_tn(d_scores, queries).astype(BF16)
        grads[2, :size, columns] = dot_tn(rounded, upstream).astype(BF16)
        if size < capacity:
            attn_all[size:, columns] = jnp.zeros((capacity - size, HEAD_DIM), BF16)

    half = capacity // 2

    @pl.when(live > half)
    def _():
        one_head(capacity)

    @pl.when(live <= half)
    def _():
        one_head(half)

    @pl.when(head == head_count - 1)
    def _():
        w_copy.wait()
        width = w_vmem.shape[1]
        step = partial.shape[1]

        def project(size):
            for first in range(0, width, step):
                total = dot_nt(grads[0, :size], w_vmem[0, first : first + step])
                total += dot_nt(grads[1, :size], w_vmem[1, first : first + step])
                total += dot_nt(grads[2, :size], w_vmem[2, first : first + step])
                partial[:size] = total
                if size < capacity:
                    partial[size:] = jnp.zeros((capacity - size, step), F32)
                for r in range(count):
                    start = pl.multiple_of((me ^ r) * rows, rows)
                    outs[r][:, first : first + step] = partial[pl.ds(start, rows)].astype(BF16)

        @pl.when(live > half)
        def _():
            project(capacity)

        @pl.when(live <= half)
        def _():
            project(half)

        for r in range(count):
            start = pl.multiple_of((me ^ r) * rows, rows)
            attn_rel[r] = attn_all[pl.ds(start, rows)]


def attend_call(slot, info, saved, d_attn, weight, count):
    capacity, width = d_attn.shape
    rows = capacity // count
    model_cols = weight.shape[1]
    heads = width // HEAD_DIM
    step = min(256, model_cols)
    return pl.pallas_call(
        functools.partial(attend_kernel, slot),
        out_shape=[jax.ShapeDtypeStruct((count, rows, width), BF16)]
        + [jax.ShapeDtypeStruct((rows, model_cols), BF16)] * count,
        grid_spec=pltpu.PrefetchScalarGridSpec(
            num_scalar_prefetch=1,
            grid=(heads,),
            in_specs=[
                pl.BlockSpec((3, capacity, HEAD_DIM), lambda h, info: (0, 0, h)),
                pl.BlockSpec((capacity, HEAD_DIM), lambda h, info: (0, h)),
                pl.BlockSpec(memory_space=pl.ANY),
            ],
            out_specs=[pl.BlockSpec((count, rows, width), lambda h, info: (0, 0, 0))]
            + [pl.BlockSpec((rows, model_cols), lambda h, info: (0, 0))] * count,
            scratch_shapes=[
                pltpu.VMEM((3, capacity, width), BF16),
                pltpu.VMEM((capacity, width), BF16),
                pltpu.VMEM((capacity, step), F32),
                pltpu.VMEM(weight.shape, BF16),
                pltpu.SemaphoreType.DMA,
            ],
        ),
        compiler_params=pltpu.CompilerParams(vmem_limit_bytes=40 * 1024 * 1024),
        cost_estimate=pl.CostEstimate(
            flops=2 * capacity * width * (6 * capacity + 3 * model_cols),
            bytes_accessed=2 * (4 * capacity * width + 3 * model_cols * width + capacity * model_cols),
            transcendentals=capacity * capacity * heads,
        ),
    )(info, saved, d_attn, weight)


def norm_kernel(info, mods, tokens, d_output, *rest):
    blocks, out, d_norm = rest[:-2], rest[-2], rest[-1]
    count = len(blocks)
    width = blocks[0].shape[1]
    for k, block in enumerate(blocks):
        owner = lax.rem(info[1] + (count - k), count)
        start = pl.multiple_of(owner * width, width)
        d_norm[:, pl.ds(start, width)] = block[...].astype(F32)
    values = tokens[...].astype(F32)
    center = values - jnp.mean(values, axis=1, keepdims=True)
    inverse = lax.rsqrt(jnp.mean(center * center, axis=1, keepdims=True) + 1e-06)
    normed = center * inverse
    gained = d_norm[...] * (1.0 + mods[0:1])
    layer = inverse * (
        gained
        - jnp.mean(gained, axis=1, keepdims=True)
        - normed * jnp.mean(gained * normed, axis=1, keepdims=True)
    )
    out[...] = (d_output[...].astype(F32) + layer).astype(BF16)


def norm_call(info, mods, tokens, d_output, blocks):
    rows, width = tokens.shape
    tile = 32
    block_width = blocks[0].shape[1]
    row_spec = lambda cols: pl.BlockSpec((tile, cols), lambda t, info: (t, 0))
    return pl.pallas_call(
        norm_kernel,
        out_shape=jax.ShapeDtypeStruct((rows, width), BF16),
        grid_spec=pltpu.PrefetchScalarGridSpec(
            num_scalar_prefetch=1,
            grid=(rows // tile,),
            in_specs=[pl.BlockSpec(mods.shape, lambda t, info: (0, 0)), row_spec(width), row_spec(width)]
            + [row_spec(block_width)] * len(blocks),
            out_specs=row_spec(width),
            scratch_shapes=[pltpu.VMEM((tile, width), F32)],
        ),
        compiler_params=pltpu.CompilerParams(vmem_limit_bytes=32 * 1024 * 1024),
        cost_estimate=pl.CostEstimate(
            flops=20 * rows * width, bytes_accessed=8 * rows * width, transcendentals=0
        ),
    )(info, mods, tokens, d_output, *blocks)


def body(section_input, saved_qkv, modulation, w_qkv, w_out, lengths, student_out, teacher_target):
    section_total = lax.axis_size("section")
    seq_total = lax.axis_size("seq")
    dp_total = lax.axis_size("dp")
    section_pos = lax.axis_index("section")
    seq_pos = lax.axis_index("seq")
    dp_pos = lax.axis_index("dp")
    tokens = section_input[0, 0]
    mods = modulation[0, 0]
    shard_rows, model_width = tokens.shape
    block_cols = model_width // dp_total
    saved = saved_qkv[0, 0].transpose(1, 0, 2)
    weight = w_qkv[0].transpose(1, 0, 2)
    weight_out = w_out[0]

    def flat(section, seq, dp):
        return (section * seq_total + seq) * dp_total + dp

    def over_dp(value, steps, sections):
        pairs = [
            (flat(s, i, j), flat(s, i, (j + steps) % dp_total))
            for s in sections
            for i in range(seq_total)
            for j in range(dp_total)
        ]
        return lax.ppermute(value, AXES, pairs)

    def over_seq(value, distance, sections):
        pairs = [
            (flat(s, i, j), flat(s, i ^ distance, j))
            for s in sections
            for i in range(seq_total)
            for j in range(dp_total)
        ]
        return lax.ppermute(value, AXES, pairs)

    every = range(section_total)
    live_counts = [lengths] + [over_dp(lengths, -k, every) for k in range(1, dp_total)]
    info = jnp.concatenate([jnp.stack([seq_pos, dp_pos]).astype(jnp.int32)] + live_counts)

    positions = seq_pos * shard_rows + jnp.arange(shard_rows, dtype=jnp.int32)
    gap = student_out[0].astype(F32) - teacher_target[0].astype(F32)
    loss_grad = jnp.where((positions < lengths[0])[:, None], gap, 0.0).astype(BF16)

    def gather_saved(section):
        return [saved] + [over_dp(saved, -k, [section]) for k in range(1, dp_total)]

    def run_section(section, d_output, saved_slots):
        only = [section]
        d_branch = (mods[1] * d_output.astype(F32)).astype(BF16)
        branch_rows = [d_branch] + [over_seq(d_branch, r, only) for r in range(1, seq_total)]
        d_attn = d_attn_call(info, branch_rows, weight_out)
        d_attn_slots = [d_attn] + [over_dp(d_attn, -k, only) for k in range(1, dp_total)]
        attn_slots, home = [], []
        for k in range(dp_total):
            attn_rel, *parts = attend_call(
                k, info, saved_slots[k], d_attn_slots[k], weight, seq_total
            )
            attn_slots.append(attn_rel)
            total = parts[0].astype(F32)
            for r in range(1, seq_total):
                total = total + over_seq(parts[r], r, only).astype(F32)
            total = total.astype(BF16)
            home.append(total if k == 0 else over_dp(total, k, only))
        d_input = norm_call(info, mods, tokens, d_output, home)
        column_blocks = []
        for k in range(dp_total):
            owner = lax.rem(dp_pos + k, dp_total)
            block = lax.dynamic_slice_in_dim(d_branch, owner * block_cols, block_cols, 1)
            column_blocks.append(block if k == 0 else over_dp(block, k, only))
        ordered = [column_blocks[(dp_total - k) % dp_total] for k in range(dp_total)]
        columns = jnp.stack(ordered)
        column_rows = [columns] + [over_seq(columns, r, only) for r in range(1, seq_total)]
        branch_all = jnp.stack(column_rows, axis=1).reshape(-1, block_cols)
        attn_all = jnp.stack(attn_slots).reshape(branch_all.shape[0], -1)
        d_out = dot_tn(attn_all, branch_all).astype(BF16)
        return d_input, d_out

    saved_slots = [gather_saved(section) for section in range(section_total)]
    d_output = loss_grad
    grad_in, grad_out = None, None
    for section in reversed(range(section_total)):
        d_input, d_out = run_section(section, d_output, saved_slots[section])
        if grad_in is None:
            grad_in, grad_out = d_input, d_out
        else:
            grad_in = jnp.where(section_pos == section, d_input, grad_in)
            grad_out = jnp.where(section_pos == section, d_out, grad_out)
        if section > 0:
            pairs = [
                (flat(section, i, j), flat(section - 1, i, j))
                for i in range(seq_total)
                for j in range(dp_total)
            ]
            d_output = lax.ppermute(d_input, AXES, pairs)
    return grad_in[None, None], grad_out[None]


def solution(mesh):
    in_specs = (
        P("section", "dp", "seq", None),
        P("section", "dp", None, None, "seq"),
        P("section", "dp", None, None),
        P("section", "dp", None, "seq"),
        P("section", "seq", None),
        P("dp"),
        P("dp", "seq", None),
        P("dp", "seq", None),
    )
    out_specs = (P("section", "dp", "seq", None), P("section", "seq", "dp"))
    return jax.shard_map(body, mesh=mesh, in_specs=in_specs, out_specs=out_specs, check_vma=False)
```

```python
import functools
import math

import jax
import jax.numpy as jnp
from jax import lax
from jax.experimental import pallas as pl
from jax.experimental.pallas import tpu as pltpu
from jax.sharding import PartitionSpec as P

HEAD_DIM = 128
AXES = ("section", "seq", "dp")
F32 = jnp.float32
BF16 = jnp.bfloat16
MIB = 1024 * 1024


def dot_nt(left, right):
    return lax.dot_general(left, right, (((1,), (1,)), ((), ())), preferred_element_type=F32)


def dot_nn(left, right):
    return lax.dot_general(left, right, (((1,), (0,)), ((), ())), preferred_element_type=F32)


def dot_tn(left, right):
    return lax.dot_general(left, right, (((0,), (0,)), ((), ())), preferred_element_type=F32)


def d_attn_kernel(info, *refs):
    blocks, w_out, out, total = refs[:-3], refs[-3], refs[-2], refs[-1]
    rows = blocks[0].shape[0]
    step = pl.program_id(0)

    @pl.when(step == 0)
    def _():
        total[...] = jnp.zeros_like(total)

    for r, block in enumerate(blocks):
        total[r * rows : (r + 1) * rows] += dot_nt(block[...], w_out[...])

    @pl.when(step == pl.num_programs(0) - 1)
    def _():
        for r in range(len(blocks)):
            start = pl.multiple_of((info[0] ^ r) * rows, rows)
            out[pl.ds(start, rows), :] = total[r * rows : (r + 1) * rows].astype(BF16)


def d_attn_call(info, blocks, w_out):
    rows, width = blocks[0].shape
    heads_width = w_out.shape[0]
    count = len(blocks)
    tile = width // 4
    return pl.pallas_call(
        d_attn_kernel,
        out_shape=jax.ShapeDtypeStruct((rows * count, heads_width), BF16),
        grid_spec=pltpu.PrefetchScalarGridSpec(
            num_scalar_prefetch=1,
            grid=(width // tile,),
            in_specs=[pl.BlockSpec((rows, tile), lambda t, info: (0, t))] * count
            + [pl.BlockSpec((heads_width, tile), lambda t, info: (0, t))],
            out_specs=pl.BlockSpec((rows * count, heads_width), lambda t, info: (0, 0)),
            scratch_shapes=[pltpu.VMEM((rows * count, heads_width), F32)],
        ),
        compiler_params=pltpu.CompilerParams(vmem_limit_bytes=32 * MIB),
        cost_estimate=pl.CostEstimate(
            flops=2 * rows * count * heads_width * width,
            bytes_accessed=2 * (rows * count * width + heads_width * width),
            transcendentals=0,
        ),
        name="d_attn",
    )(info, *blocks, w_out)


def probs_kernel(slot, info, saved, probs, mixed):
    capacity = saved.shape[1]
    live = info[2 + slot]
    factor = 1.0 / math.sqrt(HEAD_DIM)

    def one_head(size):
        queries, keys, values = saved[0, :size], saved[1, :size], saved[2, :size]
        scores = dot_nt(keys, queries) * factor
        alive = lax.broadcasted_iota(jnp.int32, (size, 1), 0) < live
        scores = jnp.where(alive, scores, -1e30)
        weights = jnp.exp(scores - jnp.max(scores, axis=0, keepdims=True))
        weights = weights * (1.0 / jnp.sum(weights, axis=0, keepdims=True))
        rounded = weights.astype(BF16)
        probs[0, :size, :size] = rounded
        mixed[:size] = dot_tn(rounded, values).astype(BF16)
        if size < capacity:
            mixed[size:] = jnp.zeros((capacity - size, HEAD_DIM), BF16)

    half = capacity // 2

    @pl.when(live > half)
    def _():
        one_head(capacity)

    @pl.when(live <= half)
    def _():
        one_head(half)


def probs_call(slot, info, saved):
    _, capacity, width = saved.shape
    heads = width // HEAD_DIM
    return pl.pallas_call(
        functools.partial(probs_kernel, slot),
        out_shape=[
            jax.ShapeDtypeStruct((heads, capacity, capacity), BF16),
            jax.ShapeDtypeStruct((capacity, width), BF16),
        ],
        grid_spec=pltpu.PrefetchScalarGridSpec(
            num_scalar_prefetch=1,
            grid=(heads,),
            in_specs=[pl.BlockSpec((3, capacity, HEAD_DIM), lambda h, info: (0, 0, h))],
            out_specs=[
                pl.BlockSpec((1, capacity, capacity), lambda h, info: (h, 0, 0)),
                pl.BlockSpec((capacity, HEAD_DIM), lambda h, info: (0, h)),
            ],
        ),
        compiler_params=pltpu.CompilerParams(vmem_limit_bytes=32 * MIB),
        cost_estimate=pl.CostEstimate(
            flops=4 * capacity * capacity * width,
            bytes_accessed=2 * (4 * capacity * width + heads * capacity * capacity),
            transcendentals=capacity * capacity * heads,
        ),
        name="probs",
    )(info, saved)


def attend_kernel(slot, info, saved, probs, mixed, d_attn, weight, other, *rest):
    outs, (grads, partial, w_vmem, w_sem) = rest[:-4], rest[-4:]
    count = len(outs)
    rows = outs[0].shape[0]
    capacity = d_attn.shape[0]
    block = weight.shape[1]
    head = pl.program_id(0)
    me, live = info[0], info[2 + slot]
    factor = 1.0 / math.sqrt(HEAD_DIM)
    copies = [
        pltpu.make_async_copy(weight, w_vmem.at[:, :block], w_sem.at[0]),
        pltpu.make_async_copy(other, w_vmem.at[:, block:], w_sem.at[1]),
    ]

    @pl.when(head == 0)
    def _():
        for copy in copies:
            copy.start()

    columns = pl.ds(pl.multiple_of(head * HEAD_DIM, HEAD_DIM), HEAD_DIM)

    def one_head(size):
        queries, keys, values = saved[0, :size], saved[1, :size], saved[2, :size]
        upstream = d_attn[:size]
        weights = probs[0, :size, :size]
        product = upstream.astype(F32) * mixed[:size].astype(F32)
        delta = jnp.sum(product.T, axis=0, keepdims=True)
        d_weights = dot_nt(values, upstream)
        d_scores = (weights.astype(F32) * (d_weights - delta) * factor).astype(BF16)
        grads[0, :size, columns] = dot_tn(d_scores, keys).astype(BF16)
        grads[1, :size, columns] = dot_nn(d_scores, queries).astype(BF16)
        grads[2, :size, columns] = dot_nn(weights, upstream).astype(BF16)

    half = capacity // 2

    @pl.when(live > half)
    def _():
        one_head(capacity)

    @pl.when(live <= half)
    def _():
        one_head(half)

    @pl.when(head == pl.num_programs(0) - 1)
    def _():
        for copy in copies:
            copy.wait()
        step = partial.shape[1]

        def project(size):
            for first in range(0, 2 * block, step):
                total = dot_nt(grads[0, :size], w_vmem[0, first : first + step])
                total += dot_nt(grads[1, :size], w_vmem[1, first : first + step])
                total += dot_nt(grads[2, :size], w_vmem[2, first : first + step])
                partial[:size] = total
                if size < capacity:
                    partial[size:] = jnp.zeros((capacity - size, step), F32)
                for r in range(count):
                    start = pl.multiple_of((me ^ r) * rows, rows)
                    outs[r][:, first : first + step] = partial[pl.ds(start, rows)].astype(BF16)

        @pl.when(live > half)
        def _():
            project(capacity)

        @pl.when(live <= half)
        def _():
            project(half)


def attend_call(slot, info, saved, probs, mixed, d_attn, weight, other, count):
    capacity, width = d_attn.shape
    rows = capacity // count
    model_cols = 2 * weight.shape[1]
    heads = width // HEAD_DIM
    step = min(512, model_cols)
    return pl.pallas_call(
        functools.partial(attend_kernel, slot),
        out_shape=[jax.ShapeDtypeStruct((rows, model_cols), BF16)] * count,
        grid_spec=pltpu.PrefetchScalarGridSpec(
            num_scalar_prefetch=1,
            grid=(heads,),
            in_specs=[
                pl.BlockSpec((3, capacity, HEAD_DIM), lambda h, info: (0, 0, h)),
                pl.BlockSpec((1, capacity, capacity), lambda h, info: (h, 0, 0)),
                pl.BlockSpec((capacity, HEAD_DIM), lambda h, info: (0, h)),
                pl.BlockSpec((capacity, HEAD_DIM), lambda h, info: (0, h)),
                pl.BlockSpec(memory_space=pl.ANY),
                pl.BlockSpec(memory_space=pl.ANY),
            ],
            out_specs=[pl.BlockSpec((rows, model_cols), lambda h, info: (0, 0))] * count,
            scratch_shapes=[
                pltpu.VMEM((3, capacity, width), BF16),
                pltpu.VMEM((capacity, step), F32),
                pltpu.VMEM((3, model_cols, width), BF16),
                pltpu.SemaphoreType.DMA((2,)),
            ],
        ),
        compiler_params=pltpu.CompilerParams(vmem_limit_bytes=40 * MIB),
        cost_estimate=pl.CostEstimate(
            flops=2 * capacity * width * (4 * capacity + 3 * model_cols),
            bytes_accessed=2 * (5 * capacity * width + 3 * model_cols * width + capacity * model_cols),
            transcendentals=0,
        ),
        name="attend",
    )(info, saved, probs, mixed, d_attn, weight, other)


def norm_kernel(info, mods, tokens, d_output, *rest):
    blocks, out, d_norm = rest[:-2], rest[-2], rest[-1]
    count = 2 * len(blocks)
    width = blocks[0].shape[1] // 2
    for k, block in enumerate(blocks):
        owner = lax.rem(info[1] + (count - 2 * k), count)
        for part in range(2):
            start = pl.multiple_of((owner ^ part) * width, width)
            d_norm[:, pl.ds(start, width)] = block[:, part * width : (part + 1) * width].astype(F32)
    values = tokens[...].astype(F32)
    center = values - jnp.mean(values, axis=1, keepdims=True)
    inverse = lax.rsqrt(jnp.mean(center * center, axis=1, keepdims=True) + 1e-06)
    normed = center * inverse
    gained = d_norm[...] * (1.0 + mods[0:1])
    layer = inverse * (
        gained
        - jnp.mean(gained, axis=1, keepdims=True)
        - normed * jnp.mean(gained * normed, axis=1, keepdims=True)
    )
    out[...] = (d_output[...].astype(F32) + layer).astype(BF16)


def norm_call(info, mods, tokens, d_output, blocks):
    rows, width = tokens.shape
    tile = 32
    block_width = blocks[0].shape[1]
    row_spec = lambda cols: pl.BlockSpec((tile, cols), lambda t, info: (t, 0))
    return pl.pallas_call(
        norm_kernel,
        out_shape=jax.ShapeDtypeStruct((rows, width), BF16),
        grid_spec=pltpu.PrefetchScalarGridSpec(
            num_scalar_prefetch=1,
            grid=(rows // tile,),
            in_specs=[pl.BlockSpec(mods.shape, lambda t, info: (0, 0)), row_spec(width), row_spec(width)]
            + [row_spec(block_width)] * len(blocks),
            out_specs=row_spec(width),
            scratch_shapes=[pltpu.VMEM((tile, width), F32)],
        ),
        compiler_params=pltpu.CompilerParams(vmem_limit_bytes=32 * MIB),
        cost_estimate=pl.CostEstimate(
            flops=20 * rows * width, bytes_accessed=8 * rows * width, transcendentals=0
        ),
        name="norm",
    )(info, mods, tokens, d_output, *blocks)


def outer_kernel(count, info, *refs):
    slots = (len(refs) - 1) // (count + 1)
    mixed, branches, out = refs[:slots], refs[slots:-1], refs[-1]
    rows = branches[0].shape[0]
    total = None
    for slot in range(slots):
        for r in range(count):
            start = pl.multiple_of((info[0] ^ r) * rows, rows)
            term = dot_tn(mixed[slot][pl.ds(start, rows), :], branches[slot * count + r][...])
            total = term if total is None else total + term
    out[...] = total.astype(BF16)


def outer_call(part, info, mixed, own_rows, other_rows, block_cols):
    capacity, width = mixed[0].shape
    count = len(own_rows)
    rows = capacity // count
    tile = min(512, block_cols)
    per_block = block_cols // tile
    slots = len(mixed)

    def own_map(t, info):
        return (0, (info[1] ^ part) * per_block + t)

    def other_map(t, info):
        return (0, part * per_block + t)

    flat_others = [rows_ for slot in other_rows for rows_ in slot]
    return pl.pallas_call(
        functools.partial(outer_kernel, count),
        out_shape=jax.ShapeDtypeStruct((width, block_cols), BF16),
        grid_spec=pltpu.PrefetchScalarGridSpec(
            num_scalar_prefetch=1,
            grid=(per_block,),
            in_specs=[pl.BlockSpec((capacity, width), lambda t, info: (0, 0))] * slots
            + [pl.BlockSpec((rows, tile), own_map)] * count
            + [pl.BlockSpec((rows, tile), other_map)] * len(flat_others),
            out_specs=pl.BlockSpec((width, tile), lambda t, info: (0, t)),
        ),
        compiler_params=pltpu.CompilerParams(vmem_limit_bytes=32 * MIB),
        cost_estimate=pl.CostEstimate(
            flops=2 * slots * capacity * width * block_cols,
            bytes_accessed=2 * (slots * capacity * (width + block_cols) + width * block_cols),
            transcendentals=0,
        ),
        name="outer",
    )(info, *mixed, *own_rows, *flat_others)


def after(value, token):
    return lax.optimization_barrier((value, token))[0]


def body(section_input, saved_qkv, modulation, w_qkv, w_out, lengths, student_out, teacher_target):
    section_total = lax.axis_size("section")
    seq_total = lax.axis_size("seq")
    dp_total = lax.axis_size("dp")
    slots = dp_total // 2
    section_pos = lax.axis_index("section")
    seq_pos = lax.axis_index("seq")
    dp_pos = lax.axis_index("dp")
    tokens = section_input[0, 0]
    mods = modulation[0, 0]
    shard_rows, model_width = tokens.shape
    block_cols = model_width // dp_total
    saved = saved_qkv[0, 0].transpose(1, 0, 2)
    weight = w_qkv[0].transpose(1, 0, 2)
    weight_out = w_out[0]

    def flat(section, seq, dp):
        return (section * seq_total + seq) * dp_total + dp

    def moved(value, sections, target):
        pairs = [
            (flat(s, i, j), flat(*target(s, i, j)))
            for s in sections
            for i in range(seq_total)
            for j in range(dp_total)
        ]
        return lax.ppermute(value, AXES, pairs)

    def over_dp(value, steps, sections):
        return moved(value, sections, lambda s, i, j: (s, i, (j + steps) % dp_total))

    def dp_pair(value, sections):
        return moved(value, sections, lambda s, i, j: (s, i, j ^ 1))

    def over_seq(value, distance, sections):
        return moved(value, sections, lambda s, i, j: (s, i ^ distance, j))

    def section_down(value, section):
        return moved(value, [section], lambda s, i, j: (s - 1, i, j))

    every = range(section_total)
    live_counts = [lengths] + [over_dp(lengths, -2 * k, every) for k in range(1, slots)]
    info = jnp.concatenate([jnp.stack([seq_pos, dp_pos]).astype(jnp.int32)] + live_counts)

    positions = seq_pos * shard_rows + jnp.arange(shard_rows, dtype=jnp.int32)
    gap = student_out[0].astype(F32) - teacher_target[0].astype(F32)
    loss_grad = jnp.where((positions < lengths[0])[:, None], gap, 0.0).astype(BF16)

    def prefetch(section, saved, weight):
        others = [over_dp(saved, -2 * k, [section]) for k in range(1, slots)]
        return others, dp_pair(weight, [section])

    def column_pair(rows, owner):
        first = lax.dynamic_slice_in_dim(rows, owner * block_cols, block_cols, 1)
        second = lax.dynamic_slice_in_dim(rows, (owner ^ 1) * block_cols, block_cols, 1)
        return jnp.concatenate([first, second], axis=1)

    own_probs = probs_call(0, info, saved)

    def run_section(section, d_output, prefetched):
        only = [section]
        saved_others, weight_other = prefetched
        d_branch = (mods[1] * d_output.astype(F32)).astype(BF16)
        own_rows = [d_branch] + [over_seq(d_branch, r, only) for r in range(1, seq_total)]
        d_attn = d_attn_call(info, own_rows, weight_out)
        d_attns = [d_attn] + [over_dp(d_attn, -2 * k, only) for k in range(1, slots)]
        gate = d_attns[-1]
        saved_slots = [saved] + saved_others
        probs_slots = [own_probs] + [probs_call(k, info, saved_slots[k]) for k in range(1, slots)]
        home = []
        for k in range(slots):
            probs, mixed = probs_slots[k]
            parts = attend_call(
                k, info, saved_slots[k], probs, mixed, d_attns[k], weight, weight_other, seq_total
            )
            total = parts[0].astype(F32)
            for r in range(1, seq_total):
                total = total + over_seq(parts[r], r, only).astype(F32)
            total = total.astype(BF16)
            home.append(total if k == 0 else over_dp(total, 2 * k, only))
        d_input = norm_call(info, mods, tokens, d_output, home)
        other_rows = []
        for k in range(1, slots):
            owner = lax.rem(dp_pos + (dp_total - 2 * k), dp_total)
            columns = over_dp(column_pair(d_branch, owner), -2 * k, only)
            other_rows.append([columns] + [over_seq(columns, r, only) for r in range(1, seq_total)])
        all_mixed = [mixed for _, mixed in probs_slots]
        sent = outer_call(1, info, all_mixed, own_rows, other_rows, block_cols)
        received = dp_pair(sent, only)
        kept = outer_call(0, info, all_mixed, own_rows, other_rows, block_cols)
        d_out = (kept.astype(F32) + received.astype(F32)).astype(BF16)
        return d_input, d_out, gate

    d_output = loss_grad
    grad_in, grad_out = None, None
    prefetched = prefetch(section_total - 1, saved, weight)
    for section in reversed(range(section_total)):
        d_input, d_out, gate = run_section(section, d_output, prefetched)
        if grad_in is None:
            grad_in, grad_out = d_input, d_out
        else:
            grad_in = jnp.where(section_pos == section, d_input, grad_in)
            grad_out = jnp.where(section_pos == section, d_out, grad_out)
        if section > 0:
            token = section_down(gate[:16, :128], section)
            prefetched = prefetch(section - 1, after(saved, token), after(weight, token))
            d_output = section_down(d_input, section)
    return grad_in[None, None], grad_out[None]


def solution(mesh):
    in_specs = (
        P("section", "dp", "seq", None),
        P("section", "dp", None, None, "seq"),
        P("section", "dp", None, None),
        P("section", "dp", None, "seq"),
        P("section", "seq", None),
        P("dp"),
        P("dp", "seq", None),
        P("dp", "seq", None),
    )
    out_specs = (P("section", "dp", "seq", None), P("section", "seq", "dp"))
    return jax.shard_map(body, mesh=mesh, in_specs=in_specs, out_specs=out_specs, check_vma=False)
```

```python
import functools
import math

import jax
import jax.numpy as jnp
from jax import lax
from jax.experimental import pallas as pl
from jax.experimental.pallas import tpu as pltpu
from jax.sharding import PartitionSpec as P

HEAD_DIM = 128
AXES = ("section", "seq", "dp")
F32 = jnp.float32
BF16 = jnp.bfloat16
MIB = 1024 * 1024
TAIL = 16
SMALL = pl.CostEstimate(flops=1024, bytes_accessed=1024, transcendentals=0)


def dot_nt(left, right):
    return lax.dot_general(left, right, (((1,), (1,)), ((), ())), preferred_element_type=F32)


def dot_nn(left, right):
    return lax.dot_general(left, right, (((1,), (0,)), ((), ())), preferred_element_type=F32)


def dot_tn(left, right):
    return lax.dot_general(left, right, (((0,), (0,)), ((), ())), preferred_element_type=F32)


def d_attn_kernel(info, *refs):
    blocks, w_out, out, joined, total = refs[:-4], refs[-4], refs[-3], refs[-2], refs[-1]
    rows = blocks[0].shape[0]
    step = pl.program_id(0)
    for r, block in enumerate(blocks):
        start = pl.multiple_of((info[0] ^ r) * rows, rows)
        joined[pl.ds(start, rows), :] = block[...]
    term = dot_nt(joined[...], w_out[...])

    @pl.when(step == 0)
    def _():
        total[...] = term

    @pl.when(step > 0)
    def _():
        total[...] += term

    @pl.when(step == pl.num_programs(0) - 1)
    def _():
        out[...] = total[...].astype(BF16)


def d_attn_call(info, blocks, w_out):
    rows, width = blocks[0].shape
    heads_width = w_out.shape[0]
    count = len(blocks)
    tile = width // 4
    return pl.pallas_call(
        d_attn_kernel,
        out_shape=jax.ShapeDtypeStruct((rows * count, heads_width), BF16),
        grid_spec=pltpu.PrefetchScalarGridSpec(
            num_scalar_prefetch=1,
            grid=(width // tile,),
            in_specs=[pl.BlockSpec((rows, tile), lambda t, info: (0, t))] * count
            + [pl.BlockSpec((heads_width, tile), lambda t, info: (0, t))],
            out_specs=pl.BlockSpec((rows * count, heads_width), lambda t, info: (0, 0)),
            scratch_shapes=[
                pltpu.VMEM((rows * count, tile), BF16),
                pltpu.VMEM((rows * count, heads_width), F32),
            ],
        ),
        compiler_params=pltpu.CompilerParams(vmem_limit_bytes=16 * MIB),
        cost_estimate=SMALL,
        name="d_attn",
    )(info, *blocks, w_out)


def live_count(tail):
    row = tail[0, 0:1, :].astype(F32)
    lane = lax.broadcasted_iota(jnp.int32, row.shape, 1)
    return jnp.sum(row * jnp.where(lane == 0, 256.0, 1.0)).astype(jnp.int32)


def tail_spec(capacity):
    return pl.BlockSpec((1, TAIL, HEAD_DIM), lambda h, info: (0, capacity // TAIL, 0))


def probs_kernel(info, saved, tail, probs, mixed):
    capacity = mixed.shape[0]
    live = live_count(tail)
    factor = 1.0 / math.sqrt(HEAD_DIM)

    def one_head(size):
        queries, keys, values = saved[0, :size], saved[1, :size], saved[2, :size]
        scores = dot_nt(keys, queries) * factor
        alive = lax.broadcasted_iota(jnp.int32, (size, 1), 0) < live
        scores = jnp.where(alive, scores, -1e30)
        weights = jnp.exp(scores - jnp.max(scores, axis=0, keepdims=True))
        weights = weights * (1.0 / jnp.sum(weights, axis=0, keepdims=True))
        rounded = weights.astype(BF16)
        probs[0, :size, :size] = rounded
        mixed[:size] = dot_tn(rounded, values).astype(BF16)
        if size < capacity:
            mixed[size:] = jnp.zeros((capacity - size, HEAD_DIM), BF16)

    half = capacity // 2

    @pl.when(live > half)
    def _():
        one_head(capacity)

    @pl.when(live <= half)
    def _():
        one_head(half)


def probs_call(info, saved, capacity):
    width = saved.shape[2]
    heads = width // HEAD_DIM
    return pl.pallas_call(
        probs_kernel,
        out_shape=[
            jax.ShapeDtypeStruct((heads, capacity, capacity), BF16),
            jax.ShapeDtypeStruct((capacity, width), BF16),
        ],
        grid_spec=pltpu.PrefetchScalarGridSpec(
            num_scalar_prefetch=1,
            grid=(heads,),
            in_specs=[
                pl.BlockSpec((3, capacity, HEAD_DIM), lambda h, info: (0, 0, h)),
                tail_spec(capacity),
            ],
            out_specs=[
                pl.BlockSpec((1, capacity, capacity), lambda h, info: (h, 0, 0)),
                pl.BlockSpec((capacity, HEAD_DIM), lambda h, info: (0, h)),
            ],
        ),
        compiler_params=pltpu.CompilerParams(vmem_limit_bytes=16 * MIB),
        cost_estimate=SMALL,
        name="probs",
    )(info, saved, saved)


def attend_kernel(info, saved, tail, probs, mixed, d_attn, weight, other, *rest):
    outs, (grads, partial, w_vmem, w_sem) = rest[:-4], rest[-4:]
    count = len(outs)
    rows = outs[0].shape[0]
    capacity = d_attn.shape[0]
    block = weight.shape[1]
    width = grads.shape[1] // 3
    head = pl.program_id(0)
    me, live = info[0], live_count(tail)
    factor = 1.0 / math.sqrt(HEAD_DIM)
    copies = [
        pltpu.make_async_copy(
            source.at[part],
            w_vmem.at[pl.ds(side * block, block), pl.ds(part * width, width)],
            w_sem.at[3 * side + part],
        )
        for side, source in enumerate((weight, other))
        for part in range(3)
    ]

    @pl.when(head == 0)
    def _():
        for copy in copies:
            copy.start()

    def columns(part):
        return pl.ds(pl.multiple_of(part * width + head * HEAD_DIM, HEAD_DIM), HEAD_DIM)

    def one_head(size):
        queries, keys, values = saved[0, :size], saved[1, :size], saved[2, :size]
        upstream = d_attn[:size]
        weights = probs[0, :size, :size]
        product = upstream.astype(F32) * mixed[:size].astype(F32)
        delta = jnp.sum(product.T, axis=0, keepdims=True)
        d_weights = dot_nt(values, upstream)
        d_scores = (weights.astype(F32) * (d_weights - delta) * factor).astype(BF16)
        grads[:size, columns(0)] = dot_tn(d_scores, keys).astype(BF16)
        grads[:size, columns(1)] = dot_nn(d_scores, queries).astype(BF16)
        grads[:size, columns(2)] = dot_nn(weights, upstream).astype(BF16)

    half = capacity // 2

    @pl.when(live > half)
    def _():
        one_head(capacity)

    @pl.when(live <= half)
    def _():
        one_head(half)

    @pl.when(head == pl.num_programs(0) - 1)
    def _():
        for copy in copies:
            copy.wait()
        step = partial.shape[1]

        def project(size):
            for first in range(0, 2 * block, step):
                partial[:size] = dot_nt(grads[:size], w_vmem[first : first + step])
                if size < capacity:
                    partial[size:] = jnp.zeros((capacity - size, step), F32)
                for r in range(count):
                    start = pl.multiple_of((me ^ r) * rows, rows)
                    outs[r][:, first : first + step] = partial[pl.ds(start, rows)].astype(BF16)

        @pl.when(live > half)
        def _():
            project(capacity)

        @pl.when(live <= half)
        def _():
            project(half)


def attend_call(info, saved, probs, mixed, d_attn, weight, other, count):
    capacity, width = d_attn.shape
    rows = capacity // count
    model_cols = 2 * weight.shape[1]
    heads = width // HEAD_DIM
    step = min(512, model_cols)
    return pl.pallas_call(
        attend_kernel,
        out_shape=[jax.ShapeDtypeStruct((rows, model_cols), BF16)] * count,
        grid_spec=pltpu.PrefetchScalarGridSpec(
            num_scalar_prefetch=1,
            grid=(heads,),
            in_specs=[
                pl.BlockSpec((3, capacity, HEAD_DIM), lambda h, info: (0, 0, h)),
                tail_spec(capacity),
                pl.BlockSpec((1, capacity, capacity), lambda h, info: (h, 0, 0)),
                pl.BlockSpec((capacity, HEAD_DIM), lambda h, info: (0, h)),
                pl.BlockSpec((capacity, HEAD_DIM), lambda h, info: (0, h)),
                pl.BlockSpec(memory_space=pl.ANY),
                pl.BlockSpec(memory_space=pl.ANY),
            ],
            out_specs=[pl.BlockSpec((rows, model_cols), lambda h, info: (0, 0))] * count,
            scratch_shapes=[
                pltpu.VMEM((capacity, 3 * width), BF16),
                pltpu.VMEM((capacity, step), F32),
                pltpu.VMEM((model_cols, 3 * width), BF16),
                pltpu.SemaphoreType.DMA((6,)),
            ],
        ),
        compiler_params=pltpu.CompilerParams(vmem_limit_bytes=24 * MIB),
        cost_estimate=SMALL,
        name="attend",
    )(info, saved, saved, probs, mixed, d_attn, weight, other)


def norm_kernel(pair, offsets, last, info, mods, tokens, d_output, extra, *rest):
    blocks, outs, d_norm = rest[: len(offsets)], rest[len(offsets) : -1], rest[-1]
    width = blocks[0].shape[1] // 2
    for offset, block in zip(offsets, blocks):
        owner = info[1] ^ offset
        for part in range(2):
            start = pl.multiple_of((owner ^ (part * pair)) * width, width)
            d_norm[:, pl.ds(start, width)] = block[:, part * width : (part + 1) * width].astype(F32)
    values = tokens[...].astype(F32)
    center = values - jnp.mean(values, axis=1, keepdims=True)
    inverse = lax.rsqrt(jnp.mean(center * center, axis=1, keepdims=True) + 1e-06)
    normed = center * inverse
    gained = d_norm[...] * (1.0 + mods[0:1])
    layer = inverse * (
        gained
        - jnp.mean(gained, axis=1, keepdims=True)
        - normed * jnp.mean(gained * normed, axis=1, keepdims=True)
    )
    d_input = (d_output[...].astype(F32) + layer).astype(BF16)
    if last:
        outs[0][...] = jnp.where(info[2] == 0, d_input, extra[...])
    else:
        outs[0][...] = d_input
        outs[1][...] = (extra[1:2] * d_input.astype(F32)).astype(BF16)


def norm_call(info, pair, offsets, mods, tokens, d_output, extra, blocks, last):
    rows, width = tokens.shape
    tile = 64
    block_width = blocks[0].shape[1]
    row_spec = lambda cols: pl.BlockSpec((tile, cols), lambda t, info: (t, 0))
    mods_spec = pl.BlockSpec(mods.shape, lambda t, info: (0, 0))
    outs = 1 if last else 2
    return pl.pallas_call(
        functools.partial(norm_kernel, pair, offsets, last),
        out_shape=[jax.ShapeDtypeStruct((rows, width), BF16)] * outs,
        grid_spec=pltpu.PrefetchScalarGridSpec(
            num_scalar_prefetch=1,
            grid=(rows // tile,),
            in_specs=[mods_spec, row_spec(width), row_spec(width), row_spec(width) if last else mods_spec]
            + [row_spec(block_width)] * len(blocks),
            out_specs=[row_spec(width)] * outs,
            scratch_shapes=[pltpu.VMEM((tile, width), F32)],
        ),
        compiler_params=pltpu.CompilerParams(vmem_limit_bytes=20 * MIB),
        cost_estimate=SMALL,
        name="norm",
    )(info, mods, tokens, d_output, extra, *blocks)


def outer_kernel(info, mixed, *refs):
    blocks, out, joined = refs[:-2], refs[-2], refs[-1]
    rows = blocks[0].shape[0]
    for r, block in enumerate(blocks):
        start = pl.multiple_of((info[0] ^ r) * rows, rows)
        joined[pl.ds(start, rows), :] = block[...]
    out[0] = dot_tn(mixed[...], joined[...]).astype(BF16)


def outer_call(parity, info, mixed, blocks, block_cols):
    capacity, width = mixed.shape
    rows, model_width = blocks[0].shape
    tile = min(512, block_cols)
    per_block = block_cols // tile
    half = model_width // block_cols // 2

    def column_map(b, t, info):
        return (0, (info[1] ^ (2 * b + parity)) * per_block + t)

    return pl.pallas_call(
        outer_kernel,
        out_shape=jax.ShapeDtypeStruct((half, width, block_cols), BF16),
        grid_spec=pltpu.PrefetchScalarGridSpec(
            num_scalar_prefetch=1,
            grid=(half, per_block),
            in_specs=[pl.BlockSpec((capacity, width), lambda b, t, info: (0, 0))]
            + [pl.BlockSpec((rows, tile), column_map)] * len(blocks),
            out_specs=pl.BlockSpec((1, width, tile), lambda b, t, info: (b, 0, t)),
            scratch_shapes=[pltpu.VMEM((capacity, tile), BF16)],
        ),
        compiler_params=pltpu.CompilerParams(vmem_limit_bytes=16 * MIB),
        cost_estimate=SMALL,
        name="outer",
    )(info, mixed, *blocks)


def after(value, *tokens):
    return lax.optimization_barrier((value, *tokens))[0]


def body(section_input, saved_qkv, modulation, w_qkv, w_out, lengths, student_out, teacher_target):
    section_total = lax.axis_size("section")
    seq_total = lax.axis_size("seq")
    dp_total = lax.axis_size("dp")
    section_pos = lax.axis_index("section")
    seq_pos = lax.axis_index("seq")
    dp_pos = lax.axis_index("dp")
    tokens = section_input[0, 0]
    mods = modulation[0, 0]
    shard_rows, model_width = tokens.shape
    capacity = saved_qkv.shape[2]
    block_cols = model_width // dp_total
    saved = saved_qkv[0, 0].transpose(1, 0, 2)
    weight = w_qkv[0].transpose(1, 0, 2)
    weight_out = w_out[0]

    def flat(section, seq, dp):
        return (section * seq_total + seq) * dp_total + dp

    def moved(value, sections, target):
        pairs = [
            (flat(s, i, j), flat(*target(s, i, j)))
            for s in sections
            for i in range(seq_total)
            for j in range(dp_total)
        ]
        return lax.ppermute(value, AXES, pairs)

    def over_dp(value, offset, sections, steps_down=0):
        return moved(value, sections, lambda s, i, j: (s - steps_down, i, j ^ offset))

    def over_seq(value, offset, sections):
        return moved(value, sections, lambda s, i, j: (s, i ^ offset, j))

    def section_shift(value, section, steps):
        return moved(value, [section], lambda s, i, j: (s + steps, i, j))

    def pair_of(section):
        return 1

    def offsets_of(section):
        return [e for e in range(dp_total) if e & pair_of(section) == 0]

    info = jnp.stack([seq_pos, dp_pos, section_pos]).astype(jnp.int32)
    positions = seq_pos * shard_rows + jnp.arange(shard_rows, dtype=jnp.int32)
    gap = student_out[0].astype(F32) - teacher_target[0].astype(F32)
    loss_grad = jnp.where((positions < lengths[0])[:, None], gap, 0.0).astype(BF16)

    def prefetch(section, saved, weight):
        others = [over_dp(saved, e, [section]) for e in offsets_of(section)[1:]]
        return others, over_dp(weight, pair_of(section), [section])

    def halve(sent, kept, offset, section):
        received = over_dp(sent, offset, [section])
        total = kept.astype(F32) + received.astype(F32)
        if total.shape[0] == 1:
            return None, total[0].astype(BF16)
        return total[1::2].astype(BF16), total[0::2]

    def finish(sent, kept, section):
        offset = 2
        while sent is not None:
            sent, kept = halve(sent, kept, offset, section)
            offset *= 2
        return kept

    def slots_of(saved_others):
        saved_slots = [saved_sent] + saved_others
        probs_slots = [own_probs] + [
            probs_call(info, saved_slots[k], capacity) for k in range(1, len(saved_slots))
        ]
        return saved_slots, probs_slots

    top = section_total - 1
    d_output = loss_grad
    d_branch = (mods[1] * d_output.astype(F32)).astype(BF16)
    high, low = lengths[0] // 256, lengths[0] % 256
    tail = jnp.zeros((3, TAIL, saved.shape[2]), BF16)
    tail = tail.at[0, 0, 0].set((high).astype(BF16))
    tail = tail.at[0, 0, 1].set((low).astype(BF16))
    saved_sent = jnp.concatenate([saved, after(tail, d_branch)], axis=1)
    prefetched = prefetch(top, saved_sent, weight)
    own_probs = probs_call(info, saved_sent, capacity)
    d_outs = [None] * section_total
    grad_up = None
    held = (own_probs[1],)
    for section in reversed(range(section_total)):
        only = [section]
        pair, offsets = pair_of(section), offsets_of(section)
        saved_others, weight_other = prefetched
        own_rows = [d_branch] + [over_seq(d_branch, r, only) for r in range(1, seq_total)]
        if section < top:
            saved_slots, probs_slots = slots_of(saved_others)
            held = held + (weight_other, probs_slots[-1][1])
        ready_rows = own_rows[:-1] + [after(own_rows[-1], *held)] if held else own_rows
        d_attn = d_attn_call(info, ready_rows, weight_out)
        if section == top:
            saved_slots, probs_slots = slots_of(saved_others)
        d_attns = [d_attn] + [over_dp(d_attn, e, only) for e in offsets[1:]]

        if section == top:
            order = list(range(1, len(offsets))) + [0]
            next_mods = section_shift(after(mods, *d_attns[1:]), section, -1)
            prefetched = prefetch(section - 1, after(saved_sent, next_mods), after(weight, next_mods))
            waits = (next_mods,)
        else:
            order = list(range(len(offsets)))
            sent = outer_call(1, info, own_probs[1], [after(own_rows[0], d_attn)] + own_rows[1:], block_cols)
            waits = (sent,)
        all_parts = {}
        for k in order:
            probs, mixed = probs_slots[k]
            all_parts[k] = attend_call(
                info,
                saved_slots[k],
                probs,
                mixed,
                after(d_attns[k], *waits) if waits else d_attns[k],
                weight,
                weight_other,
                seq_total,
            )
            waits = (all_parts[k][0],)
        if section > 0:
            token = all_parts[order[0]][0]
            next_tokens = section_shift(after(tokens, token), section, -1)
        last_rows = [after(own_rows[0], *waits)] + own_rows[1:]
        if section == top:
            sent = outer_call(1, info, own_probs[1], last_rows, block_cols)
        kept = outer_call(0, info, own_probs[1], last_rows, block_cols)
        down = 1 if section > 0 else 0
        home = []
        for k, e in enumerate(offsets):
            parts = all_parts[k]
            total = parts[0].astype(F32)
            for r in range(1, seq_total):
                total = total + over_seq(parts[r], r, only).astype(F32)
            total = total.astype(BF16)
            home.append(over_dp(total, e, only, down) if e or down else total)

        if section > 0:
            d_output, d_branch = norm_call(
                info, pair, offsets, next_mods, after(next_tokens, kept, sent), d_output, mods, home, False
            )
            back = section_shift(d_output, section - 1, 1)
            grad_up = back if grad_up is None else jnp.where(section_pos == section, back, grad_up)
            held = ()
            d_outs[section] = finish(*halve(sent, kept, 1, section), section)
        else:
            (grad_in,) = norm_call(
                info, pair, offsets, mods, tokens, d_output, grad_up, home, True
            )
            sent = after(sent, *d_attns[1:])
            d_outs[section] = finish(*halve(sent, kept, 1, section), section)
    grad_out = d_outs[0]
    for section in range(1, section_total):
        grad_out = jnp.where(section_pos == section, d_outs[section], grad_out)
    return grad_in[None, None], grad_out[None]


def solution(mesh):
    in_specs = (
        P("section", "dp", "seq", None),
        P("section", "dp", None, None, "seq"),
        P("section", "dp", None, None),
        P("section", "dp", None, "seq"),
        P("section", "seq", None),
        P("dp"),
        P("dp", "seq", None),
        P("dp", "seq", None),
    )
    out_specs = (P("section", "dp", "seq", None), P("section", "seq", "dp"))
    return jax.shard_map(body, mesh=mesh, in_specs=in_specs, out_specs=out_specs, check_vma=False)
```

```python
import functools
import math

import jax
import jax.numpy as jnp
from jax import lax
from jax.experimental import pallas as pl
from jax.experimental.pallas import tpu as pltpu
from jax.sharding import PartitionSpec as P

HEAD_DIM = 128
AXES = ("section", "seq", "dp")
F32 = jnp.float32
BF16 = jnp.bfloat16
MIB = 1024 * 1024
TAIL = 16
SMALL = pl.CostEstimate(flops=1024, bytes_accessed=1024, transcendentals=0)


def dot_nt(left, right):
    return lax.dot_general(left, right, (((1,), (1,)), ((), ())), preferred_element_type=F32)


def dot_nn(left, right):
    return lax.dot_general(left, right, (((1,), (0,)), ((), ())), preferred_element_type=F32)


def dot_tn(left, right):
    return lax.dot_general(left, right, (((0,), (0,)), ((), ())), preferred_element_type=F32)


def d_attn_kernel(info, *refs):
    blocks, w_out, out, joined, total = refs[:-4], refs[-4], refs[-3], refs[-2], refs[-1]
    rows = blocks[0].shape[0]
    step = pl.program_id(0)
    for r, block in enumerate(blocks):
        start = pl.multiple_of((info[0] ^ r) * rows, rows)
        joined[pl.ds(start, rows), :] = block[...]
    term = dot_nt(joined[...], w_out[...])

    @pl.when(step == 0)
    def _():
        total[...] = term

    @pl.when(step > 0)
    def _():
        total[...] += term

    @pl.when(step == pl.num_programs(0) - 1)
    def _():
        out[...] = total[...].astype(BF16)


def d_attn_call(info, blocks, w_out):
    rows, width = blocks[0].shape
    heads_width = w_out.shape[0]
    count = len(blocks)
    tile = width // 4
    return pl.pallas_call(
        d_attn_kernel,
        out_shape=jax.ShapeDtypeStruct((rows * count, heads_width), BF16),
        grid_spec=pltpu.PrefetchScalarGridSpec(
            num_scalar_prefetch=1,
            grid=(width // tile,),
            in_specs=[pl.BlockSpec((rows, tile), lambda t, info: (0, t))] * count
            + [pl.BlockSpec((heads_width, tile), lambda t, info: (0, t))],
            out_specs=pl.BlockSpec((rows * count, heads_width), lambda t, info: (0, 0)),
            scratch_shapes=[
                pltpu.VMEM((rows * count, tile), BF16),
                pltpu.VMEM((rows * count, heads_width), F32),
            ],
        ),
        compiler_params=pltpu.CompilerParams(vmem_limit_bytes=16 * MIB),
        cost_estimate=SMALL,
        name="d_attn",
    )(info, *blocks, w_out)


def live_count(tail):
    row = tail[0, 0:1, :].astype(F32)
    lane = lax.broadcasted_iota(jnp.int32, row.shape, 1)
    return jnp.sum(row * jnp.where(lane == 0, 256.0, 1.0)).astype(jnp.int32)


def tail_spec(capacity):
    return pl.BlockSpec((1, TAIL, HEAD_DIM), lambda h, info: (0, capacity // TAIL, 0))


def probs_kernel(info, saved, tail, probs, mixed):
    capacity = mixed.shape[0]
    live = live_count(tail)
    factor = 1.0 / math.sqrt(HEAD_DIM)

    def one_head(size):
        queries, keys, values = saved[0, :size], saved[1, :size], saved[2, :size]
        scores = dot_nt(keys, queries) * factor
        alive = lax.broadcasted_iota(jnp.int32, (size, 1), 0) < live
        scores = jnp.where(alive, scores, -1e30)
        weights = jnp.exp(scores - jnp.max(scores, axis=0, keepdims=True))
        weights = weights * (1.0 / jnp.sum(weights, axis=0, keepdims=True))
        rounded = weights.astype(BF16)
        probs[0, :size, :size] = rounded
        mixed[:size] = dot_tn(rounded, values).astype(BF16)
        if size < capacity:
            mixed[size:] = jnp.zeros((capacity - size, HEAD_DIM), BF16)

    half = capacity // 2

    @pl.when(live > half)
    def _():
        one_head(capacity)

    @pl.when(live <= half)
    def _():
        one_head(half)


def probs_call(info, saved, capacity):
    width = saved.shape[2]
    heads = width // HEAD_DIM
    return pl.pallas_call(
        probs_kernel,
        out_shape=[
            jax.ShapeDtypeStruct((heads, capacity, capacity), BF16),
            jax.ShapeDtypeStruct((capacity, width), BF16),
        ],
        grid_spec=pltpu.PrefetchScalarGridSpec(
            num_scalar_prefetch=1,
            grid=(heads,),
            in_specs=[
                pl.BlockSpec((3, capacity, HEAD_DIM), lambda h, info: (0, 0, h)),
                tail_spec(capacity),
            ],
            out_specs=[
                pl.BlockSpec((1, capacity, capacity), lambda h, info: (h, 0, 0)),
                pl.BlockSpec((capacity, HEAD_DIM), lambda h, info: (0, h)),
            ],
        ),
        compiler_params=pltpu.CompilerParams(vmem_limit_bytes=16 * MIB),
        cost_estimate=SMALL,
        name="probs",
    )(info, saved, saved)


def attend_kernel(info, saved, tail, probs, mixed, d_attn, weight, other, *rest):
    outs, (grads, partial, w_vmem, w_sem) = rest[:-4], rest[-4:]
    rows = outs[0].shape[-2]
    capacity = d_attn.shape[0]
    count = capacity // rows
    grouped = len(outs) < count
    block = weight.shape[1]
    width = grads.shape[1] // 3
    head = pl.program_id(0)
    me, live = info[0], live_count(tail)
    factor = 1.0 / math.sqrt(HEAD_DIM)
    copies = [
        pltpu.make_async_copy(
            source.at[part],
            w_vmem.at[pl.ds(side * block, block), pl.ds(part * width, width)],
            w_sem.at[3 * side + part],
        )
        for side, source in enumerate((weight, other))
        for part in range(3)
    ]

    @pl.when(head == 0)
    def _():
        for copy in copies:
            copy.start()

    def columns(part):
        return pl.ds(pl.multiple_of(part * width + head * HEAD_DIM, HEAD_DIM), HEAD_DIM)

    def one_head(size):
        queries, keys, values = saved[0, :size], saved[1, :size], saved[2, :size]
        upstream = d_attn[:size]
        weights = probs[0, :size, :size]
        product = upstream.astype(F32) * mixed[:size].astype(F32)
        delta = jnp.sum(product.T, axis=0, keepdims=True)
        d_weights = dot_nt(values, upstream)
        d_scores = (weights.astype(F32) * (d_weights - delta) * factor).astype(BF16)
        grads[:size, columns(0)] = dot_tn(d_scores, keys).astype(BF16)
        grads[:size, columns(1)] = dot_nn(d_scores, queries).astype(BF16)
        grads[:size, columns(2)] = dot_nn(weights, upstream).astype(BF16)

    half = capacity // 2

    @pl.when(live > half)
    def _():
        one_head(capacity)

    @pl.when(live <= half)
    def _():
        one_head(half)

    @pl.when(head == pl.num_programs(0) - 1)
    def _():
        for copy in copies:
            copy.wait()
        step = min(512, 2 * block)

        def project(size):
            for first in range(0, 2 * block, step):
                product = dot_nt(grads[:size], w_vmem[first : first + step])
                partial[:size, first : first + step] = product.astype(BF16)
            if size < capacity:
                partial[size:] = jnp.zeros((capacity - size, 2 * block), BF16)
            for r in range(count):
                start = pl.multiple_of((me ^ r) * rows, rows)
                block_rows = partial[pl.ds(start, rows)]
                if grouped:
                    outs[r % 2][r // 2] = block_rows
                else:
                    outs[r][...] = block_rows

        @pl.when(live > half)
        def _():
            project(capacity)

        @pl.when(live <= half)
        def _():
            project(half)


def attend_call(info, saved, probs, mixed, d_attn, weight, other, count, grouped):
    capacity, width = d_attn.shape
    rows = capacity // count
    model_cols = 2 * weight.shape[1]
    heads = width // HEAD_DIM
    if grouped:
        outs, shape = 2, (count // 2, rows, model_cols)
    else:
        outs, shape = count, (rows, model_cols)
    return pl.pallas_call(
        attend_kernel,
        out_shape=[jax.ShapeDtypeStruct(shape, BF16)] * outs,
        grid_spec=pltpu.PrefetchScalarGridSpec(
            num_scalar_prefetch=1,
            grid=(heads,),
            in_specs=[
                pl.BlockSpec((3, capacity, HEAD_DIM), lambda h, info: (0, 0, h)),
                tail_spec(capacity),
                pl.BlockSpec((1, capacity, capacity), lambda h, info: (h, 0, 0)),
                pl.BlockSpec((capacity, HEAD_DIM), lambda h, info: (0, h)),
                pl.BlockSpec((capacity, HEAD_DIM), lambda h, info: (0, h)),
                pl.BlockSpec(memory_space=pl.ANY),
                pl.BlockSpec(memory_space=pl.ANY),
            ],
            out_specs=[pl.BlockSpec(shape, lambda h, info: (0,) * len(shape))] * outs,
            scratch_shapes=[
                pltpu.VMEM((capacity, 3 * width), BF16),
                pltpu.VMEM((capacity, model_cols), BF16),
                pltpu.VMEM((model_cols, 3 * width), BF16),
                pltpu.SemaphoreType.DMA((6,)),
            ],
        ),
        compiler_params=pltpu.CompilerParams(vmem_limit_bytes=24 * MIB),
        cost_estimate=SMALL,
        name="attend",
    )(info, saved, saved, probs, mixed, d_attn, weight, other)


def norm_kernel(pair, offsets, home, info, mods, tokens, d_output, upper, *rest):
    blocks, rest = rest[: len(offsets)], rest[len(offsets) :]
    d_norm = rest[-1]
    width = blocks[0].shape[1] // 2
    for offset, block in zip(offsets, blocks):
        owner = info[1] ^ offset
        for part in range(2):
            start = pl.multiple_of((owner ^ (part * pair)) * width, width)
            d_norm[:, pl.ds(start, width)] = block[:, part * width : (part + 1) * width].astype(F32)
    values = tokens[...].astype(F32)
    center = values - jnp.mean(values, axis=1, keepdims=True)
    inverse = lax.rsqrt(jnp.mean(center * center, axis=1, keepdims=True) + 1e-06)
    normed = center * inverse
    gained = d_norm[...] * (1.0 + mods[0:1])
    layer = inverse * (
        gained
        - jnp.mean(gained, axis=1, keepdims=True)
        - normed * jnp.mean(gained * normed, axis=1, keepdims=True)
    )
    d_input = (d_output[...].astype(F32) + layer).astype(BF16)
    if len(rest) == 2:
        rest[0][...] = jnp.where(info[2] == home, d_input, upper[...])
    else:
        next_mods, out, d_branch = rest[:3]
        out[...] = d_input
        gated = (next_mods[1:2] * d_input.astype(F32)).astype(BF16)
        d_branch[...] = jnp.where(info[2] == home, gated, upper[...])


def norm_call(info, pair, offsets, home, mods, tokens, d_output, upper, blocks, next_mods=()):
    rows, width = tokens.shape
    tile = 64
    block_width = blocks[0].shape[1]
    row_spec = lambda cols: pl.BlockSpec((tile, cols), lambda t, info: (t, 0))
    mods_spec = pl.BlockSpec(mods.shape, lambda t, info: (0, 0))
    outs = 1 + len(next_mods)
    return pl.pallas_call(
        functools.partial(norm_kernel, pair, offsets, home),
        out_shape=[jax.ShapeDtypeStruct((rows, width), BF16)] * outs,
        grid_spec=pltpu.PrefetchScalarGridSpec(
            num_scalar_prefetch=1,
            grid=(rows // tile,),
            in_specs=[mods_spec, row_spec(width), row_spec(width), row_spec(width)]
            + [row_spec(block_width)] * len(blocks)
            + [mods_spec] * len(next_mods),
            out_specs=[row_spec(width)] * outs,
            scratch_shapes=[pltpu.VMEM((tile, width), F32)],
        ),
        compiler_params=pltpu.CompilerParams(vmem_limit_bytes=20 * MIB),
        cost_estimate=SMALL,
        name="norm",
    )(info, mods, tokens, d_output, upper, *blocks, *next_mods)


def outer_kernel(sections, slots, count, info, *refs):
    out, joined = refs[-2], refs[-1]
    refs = iter(refs[:-2])
    rows = joined.shape[1] // count

    def chosen(options):
        value = options[0][...]
        for section in range(1, sections):
            value = jnp.where(info[2] == section, options[section][...], value)
        return value

    def take(amount):
        return [next(refs) for _ in range(amount)]

    total = None
    for slot in range(slots):
        mixed = take(1)[0][...] if slot == 0 else chosen(take(sections))
        for r in range(count):
            start = pl.multiple_of((info[0] ^ r) * rows, rows)
            single = r == 0 or slot > 0
            joined[slot, pl.ds(start, rows), :] = (
                take(1)[0][...] if single else chosen(take(sections))
            )
        term = dot_tn(mixed, joined[slot])
        total = term if total is None else total + term
    out[...] = total.astype(BF16)


def outer_call(part, pair, info, own_mixed, other_mixed, own_rows, other_rows, block_cols):
    capacity, width = own_mixed.shape
    count = len(own_rows)
    rows = capacity // count
    tile = min(512, block_cols)
    per_block = block_cols // tile
    mixed_spec = pl.BlockSpec((capacity, width), lambda t, info: (0, 0))

    def own_map(t, info):
        return (0, (info[1] ^ (part * pair)) * per_block + t)

    def other_map(t, info):
        return (0, part * per_block + t)

    operands, specs = [own_mixed], [mixed_spec]
    for options in own_rows:
        operands += options
        specs += [pl.BlockSpec((rows, tile), own_map)] * len(options)
    for mixed, blocks in zip(other_mixed, other_rows):
        operands += mixed + blocks
        specs += [mixed_spec] * len(mixed) + [pl.BlockSpec((rows, tile), other_map)] * len(blocks)
    return pl.pallas_call(
        functools.partial(outer_kernel, len(own_rows[1]), 1 + len(other_mixed), count),
        out_shape=jax.ShapeDtypeStruct((width, block_cols), BF16),
        grid_spec=pltpu.PrefetchScalarGridSpec(
            num_scalar_prefetch=1,
            grid=(per_block,),
            in_specs=specs,
            out_specs=pl.BlockSpec((width, tile), lambda t, info: (0, t)),
            scratch_shapes=[pltpu.VMEM((1 + len(other_mixed), capacity, tile), BF16)],
        ),
        compiler_params=pltpu.CompilerParams(vmem_limit_bytes=24 * MIB),
        cost_estimate=SMALL,
        name="outer",
    )(info, *operands)


def after(value, *tokens):
    return lax.optimization_barrier((value, *tokens))[0]


def body(section_input, saved_qkv, modulation, w_qkv, w_out, lengths, student_out, teacher_target):
    section_total = lax.axis_size("section")
    seq_total = lax.axis_size("seq")
    dp_total = lax.axis_size("dp")
    section_pos = lax.axis_index("section")
    seq_pos = lax.axis_index("seq")
    dp_pos = lax.axis_index("dp")
    tokens = section_input[0, 0]
    mods = modulation[0, 0]
    shard_rows, model_width = tokens.shape
    capacity = saved_qkv.shape[2]
    block_cols = model_width // dp_total
    pair = 1
    offsets = [e for e in range(dp_total) if e & pair == 0]
    saved = saved_qkv[0, 0].transpose(1, 0, 2)
    weight = w_qkv[0].transpose(1, 0, 2)
    weight_out = w_out[0]

    def flat(section, seq, dp):
        return (section * seq_total + seq) * dp_total + dp

    def moved(value, sections, target):
        pairs = [
            (flat(s, i, j), flat(*target(s, i, j)))
            for s in sections
            for i in range(seq_total)
            for j in range(dp_total)
        ]
        return lax.ppermute(value, AXES, pairs)

    def over_dp(value, offset, sections, steps_down=0):
        return moved(value, sections, lambda s, i, j: (s - steps_down, i, j ^ offset))

    def over_seq(value, offset, sections):
        return moved(value, sections, lambda s, i, j: (s, i ^ offset, j))

    def section_shift(value, section, steps):
        return moved(value, [section], lambda s, i, j: (s + steps, i, j))

    info = jnp.stack([seq_pos, dp_pos, section_pos]).astype(jnp.int32)
    positions = seq_pos * shard_rows + jnp.arange(shard_rows, dtype=jnp.int32)
    gap = student_out[0].astype(F32) - teacher_target[0].astype(F32)
    loss_grad = jnp.where((positions < lengths[0])[:, None], gap, 0.0).astype(BF16)

    def prefetch(section, saved, weight):
        others = [over_dp(saved, e, [section]) for e in offsets[1:]]
        return others, over_dp(weight, pair, [section])

    def halved(kept, sent, sections):
        offset = 1
        while True:
            total = kept.astype(F32) + over_seq(sent, offset, sections).astype(F32)
            if total.shape[0] == 1:
                return total[0].astype(BF16)
            offset *= 2
            kept, sent = total[0::2], total[1::2].astype(BF16)

    def column_pair(rows, owner):
        first = lax.dynamic_slice_in_dim(rows, owner * block_cols, block_cols, 1)
        second = lax.dynamic_slice_in_dim(rows, (owner ^ 1) * block_cols, block_cols, 1)
        return jnp.concatenate([first, second], axis=1)

    def slots_of(saved_others):
        saved_slots = [saved_sent] + saved_others
        probs_slots = [own_probs] + [
            probs_call(info, saved_slots[k], capacity) for k in range(1, len(saved_slots))
        ]
        return saved_slots, probs_slots

    top = section_total - 1
    d_output = loss_grad
    d_branch = (mods[1] * d_output.astype(F32)).astype(BF16)
    high, low = lengths[0] // 256, lengths[0] % 256
    tail = jnp.zeros((3, TAIL, saved.shape[2]), BF16)
    tail = tail.at[0, 0, 0].set((high).astype(BF16))
    tail = tail.at[0, 0, 1].set((low).astype(BF16))
    saved_sent = jnp.concatenate([saved, tail], axis=1)
    prefetched = prefetch(top, saved_sent, after(weight, d_branch))
    own_probs = probs_call(info, saved_sent, capacity)
    grad_up = None
    held = (own_probs[1],)
    every = list(range(section_total))
    rows_of, mixed_of = [None] * section_total, [None] * section_total
    for section in reversed(every):
        only = [section]
        saved_others, weight_other = prefetched
        own_rows = [d_branch] + [over_seq(d_branch, r, only) for r in range(1, seq_total)]
        if section < top:
            saved_slots, probs_slots = slots_of(saved_others)
            held = held + (weight_other, probs_slots[-1][1])
        ready_rows = own_rows[:-1] + [after(own_rows[-1], *held)] if held else own_rows
        d_attn = d_attn_call(info, ready_rows, weight_out)
        if section == top:
            saved_slots, probs_slots = slots_of(saved_others)
        d_attns = [d_attn] + [over_dp(d_attn, e, only) for e in offsets[1:]]
        rows_of[section] = own_rows
        mixed_of[section] = [mixed for _, mixed in probs_slots[1:]]

        waits = ()
        all_parts = {}
        for k in range(len(offsets)):
            probs, mixed = probs_slots[k]
            if k == 1 and section > 0:
                ready = [mixed for _, mixed in probs_slots[1:]]
                next_mods = section_shift(after(mods, *waits, *ready, *d_attns[1:]), section, -1)
                next_saved = [
                    over_dp(after(saved_sent, next_mods), e, [section - 1]) for e in offsets[1:]
                ]
                waits = waits + (next_mods,)
            all_parts[k] = attend_call(
                info,
                saved_slots[k],
                probs,
                mixed,
                after(d_attns[k], *waits) if waits else d_attns[k],
                weight,
                weight_other,
                seq_total,
                k == 0 and section == top,
            )
            waits = (all_parts[k][0],)
        if section > 0:
            next_other = over_dp(after(weight, *waits), pair, [section - 1])
            next_tokens = section_shift(after(tokens, *waits), section, -1)
        down = 1 if section > 0 else 0
        home = []
        for k, e in enumerate(offsets):
            parts = all_parts[k]
            if k == 0 and section == top:
                total = halved(parts[0], after(parts[1], *d_attns[1:]), only)
            else:
                total = parts[0].astype(F32)
                for r in range(1, seq_total):
                    total = total + over_seq(parts[r], r, only).astype(F32)
                total = total.astype(BF16)
            home.append(over_dp(total, e, only, down) if e or down else total)

        if section > 0:
            prefetched = next_saved, next_other
            d_output, d_branch = norm_call(
                info,
                pair,
                offsets,
                section - 1,
                next_mods,
                next_tokens,
                d_output,
                d_branch,
                home,
                (mods,),
            )
            back = section_shift(d_output, section - 1, 1)
            grad_up = back if grad_up is None else jnp.where(section_pos == section, back, grad_up)
            held = ()
    (grad_in,) = norm_call(info, pair, offsets, 0, mods, tokens, d_output, grad_up, home)

    other_rows = []
    for e in offsets[1:]:
        columns = over_dp(column_pair(d_branch, dp_pos ^ e), e, every)
        other_rows.append([columns] + [over_seq(columns, r, every) for r in range(1, seq_total)])
    own_options = [[after(d_branch, *waits)]]
    own_options += [[rows_of[s][r] for s in every] for r in range(1, seq_total)]
    mixed_options = [[mixed_of[s][k] for s in every] for k in range(len(offsets) - 1)]
    sent, kept = [
        outer_call(part, pair, info, own_probs[1], mixed_options, own_options, other_rows, block_cols)
        for part in (1, 0)
    ]
    received = over_dp(sent, pair, every)
    grad_out = (kept.astype(F32) + received.astype(F32)).astype(BF16)
    return grad_in[None, None], grad_out[None]


def solution(mesh):
    in_specs = (
        P("section", "dp", "seq", None),
        P("section", "dp", None, None, "seq"),
        P("section", "dp", None, None),
        P("section", "dp", None, "seq"),
        P("section", "seq", None),
        P("dp"),
        P("dp", "seq", None),
        P("dp", "seq", None),
    )
    out_specs = (P("section", "dp", "seq", None), P("section", "seq", "dp"))
    return jax.shard_map(body, mesh=mesh, in_specs=in_specs, out_specs=out_specs, check_vma=False)
```

```python
import functools
import math

import jax
import jax.numpy as jnp
from jax import lax
from jax.experimental import pallas as pl
from jax.experimental.pallas import tpu as pltpu
from jax.sharding import PartitionSpec as P

HEAD_DIM = 128
AXES = ("section", "seq", "dp")
F32 = jnp.float32
BF16 = jnp.bfloat16
MIB = 1024 * 1024
TAIL = 16
SMALL = pl.CostEstimate(flops=1024, bytes_accessed=1024, transcendentals=0)


def dot_nt(left, right):
    return lax.dot_general(left, right, (((1,), (1,)), ((), ())), preferred_element_type=F32)


def dot_nn(left, right):
    return lax.dot_general(left, right, (((1,), (0,)), ((), ())), preferred_element_type=F32)


def dot_tn(left, right):
    return lax.dot_general(left, right, (((0,), (0,)), ((), ())), preferred_element_type=F32)


def d_attn_kernel(info, *refs):
    blocks, w_out, out, joined, total = refs[:-4], refs[-4], refs[-3], refs[-2], refs[-1]
    rows = blocks[0].shape[0]
    step = pl.program_id(0)
    for r, block in enumerate(blocks):
        start = pl.multiple_of((info[0] ^ r) * rows, rows)
        joined[pl.ds(start, rows), :] = block[...]
    term = dot_nt(joined[...], w_out[...])

    @pl.when(step == 0)
    def _():
        total[...] = term

    @pl.when(step > 0)
    def _():
        total[...] += term

    @pl.when(step == pl.num_programs(0) - 1)
    def _():
        out[...] = total[...].astype(BF16)


def d_attn_call(info, blocks, w_out):
    rows, width = blocks[0].shape
    heads_width = w_out.shape[0]
    count = len(blocks)
    tile = width // 4
    return pl.pallas_call(
        d_attn_kernel,
        out_shape=jax.ShapeDtypeStruct((rows * count, heads_width), BF16),
        grid_spec=pltpu.PrefetchScalarGridSpec(
            num_scalar_prefetch=1,
            grid=(width // tile,),
            in_specs=[pl.BlockSpec((rows, tile), lambda t, info: (0, t))] * count
            + [pl.BlockSpec((heads_width, tile), lambda t, info: (0, t))],
            out_specs=pl.BlockSpec((rows * count, heads_width), lambda t, info: (0, 0)),
            scratch_shapes=[
                pltpu.VMEM((rows * count, tile), BF16),
                pltpu.VMEM((rows * count, heads_width), F32),
            ],
        ),
        compiler_params=pltpu.CompilerParams(vmem_limit_bytes=16 * MIB),
        cost_estimate=SMALL,
        name="d_attn",
    )(info, *blocks, w_out)


def live_count(tail):
    row = tail[0, 0:1, :].astype(F32)
    lane = lax.broadcasted_iota(jnp.int32, row.shape, 1)
    return jnp.sum(row * jnp.where(lane == 0, 256.0, 1.0)).astype(jnp.int32)


def tail_spec(capacity):
    return pl.BlockSpec((1, TAIL, HEAD_DIM), lambda h, info: (0, capacity // TAIL, 0))


def probs_kernel(info, saved, tail, probs, mixed):
    capacity = mixed.shape[0]
    live = live_count(tail)
    factor = 1.0 / math.sqrt(HEAD_DIM)

    def one_head(size):
        queries, keys, values = saved[0, :size], saved[1, :size], saved[2, :size]
        scores = dot_nt(keys, queries) * factor
        alive = lax.broadcasted_iota(jnp.int32, (size, 1), 0) < live
        scores = jnp.where(alive, scores, -1e30)
        weights = jnp.exp(scores - jnp.max(scores, axis=0, keepdims=True))
        weights = weights * (1.0 / jnp.sum(weights, axis=0, keepdims=True))
        rounded = weights.astype(BF16)
        probs[0, :size, :size] = rounded
        mixed[:size] = dot_tn(rounded, values).astype(BF16)
        if size < capacity:
            mixed[size:] = jnp.zeros((capacity - size, HEAD_DIM), BF16)

    half = capacity // 2

    @pl.when(live > half)
    def _():
        one_head(capacity)

    @pl.when(live <= half)
    def _():
        one_head(half)


def probs_call(info, saved, capacity):
    width = saved.shape[2]
    heads = width // HEAD_DIM
    return pl.pallas_call(
        probs_kernel,
        out_shape=[
            jax.ShapeDtypeStruct((heads, capacity, capacity), BF16),
            jax.ShapeDtypeStruct((capacity, width), BF16),
        ],
        grid_spec=pltpu.PrefetchScalarGridSpec(
            num_scalar_prefetch=1,
            grid=(heads,),
            in_specs=[
                pl.BlockSpec((3, capacity, HEAD_DIM), lambda h, info: (0, 0, h)),
                tail_spec(capacity),
            ],
            out_specs=[
                pl.BlockSpec((1, capacity, capacity), lambda h, info: (h, 0, 0)),
                pl.BlockSpec((capacity, HEAD_DIM), lambda h, info: (0, h)),
            ],
        ),
        compiler_params=pltpu.CompilerParams(vmem_limit_bytes=16 * MIB),
        cost_estimate=SMALL,
        name="probs",
    )(info, saved, saved)


def attend_kernel(section, info, saved, tail, probs, mixed, d_attn, weight, other, *rest):
    outs, (grads, partial, w_vmem, w_sem) = rest[:-4], rest[-4:]
    rows = outs[0].shape[-2]
    capacity = d_attn.shape[0]
    count = capacity // rows
    grouped = len(outs) < count
    block = weight.shape[1]
    width = grads.shape[1] // 3
    heads = width // HEAD_DIM
    me, live, active = info[0], live_count(tail), info[2] == section
    factor = 1.0 / math.sqrt(HEAD_DIM)
    copies = [
        pltpu.make_async_copy(
            source.at[part],
            w_vmem.at[pl.ds(side * block, block), pl.ds(part * width, width)],
            w_sem.at[3 * side + part],
        )
        for side, source in enumerate((weight, other))
        for part in range(3)
    ]

    @pl.when(active)
    def _():
        for copy in copies:
            copy.start()

    def all_heads(size):
        for head in range(heads):
            one_head(size, head)

    def one_head(size, head):
        lanes = slice(head * HEAD_DIM, (head + 1) * HEAD_DIM)

        def columns(part):
            first = part * width + head * HEAD_DIM
            return slice(first, first + HEAD_DIM)

        queries, keys, values = saved[0, :size, lanes], saved[1, :size, lanes], saved[2, :size, lanes]
        upstream = d_attn[:size, lanes]
        weights = probs[head, :size, :size]
        product = upstream.astype(F32) * mixed[:size, lanes].astype(F32)
        delta = jnp.sum(product.T, axis=0, keepdims=True)
        d_weights = dot_nt(values, upstream)
        d_scores = (weights.astype(F32) * (d_weights - delta) * factor).astype(BF16)
        grads[:size, columns(0)] = dot_nn(keys.T, d_scores).T.astype(BF16)
        grads[:size, columns(1)] = dot_nn(d_scores, queries).astype(BF16)
        grads[:size, columns(2)] = dot_nn(weights, upstream).astype(BF16)

    half = capacity // 2

    @pl.when(active & (live > half))
    def _():
        all_heads(capacity)

    @pl.when(active & (live <= half))
    def _():
        all_heads(half)

    @pl.when(active)
    def _():
        for copy in copies:
            copy.wait()
        step = min(512, 2 * block)

        def project(size):
            for first in range(0, 2 * block, step):
                product = dot_nt(grads[:size], w_vmem[first : first + step])
                partial[:size, first : first + step] = product.astype(BF16)
            if size < capacity:
                partial[size:] = jnp.zeros((capacity - size, 2 * block), BF16)
            for r in range(count):
                start = pl.multiple_of((me ^ r) * rows, rows)
                block_rows = partial[pl.ds(start, rows)]
                if grouped:
                    outs[r % 2][r // 2] = block_rows
                else:
                    outs[r][...] = block_rows

        @pl.when(live > half)
        def _():
            project(capacity)

        @pl.when(live <= half)
        def _():
            project(half)


def attend_call(info, saved, probs, mixed, d_attn, weight, other, count, grouped, section):
    capacity, width = d_attn.shape
    rows = capacity // count
    model_cols = 2 * weight.shape[1]
    heads = width // HEAD_DIM
    if grouped:
        outs, shape = 2, (count // 2, rows, model_cols)
    else:
        outs, shape = count, (rows, model_cols)
    once = pl.Buffered(1)
    return pl.pallas_call(
        functools.partial(attend_kernel, section),
        out_shape=[jax.ShapeDtypeStruct(shape, BF16)] * outs,
        grid_spec=pltpu.PrefetchScalarGridSpec(
            num_scalar_prefetch=1,
            grid=(1,),
            in_specs=[
                pl.BlockSpec((3, capacity, width), lambda h, info: (0, 0, 0), pipeline_mode=once),
                tail_spec(capacity),
                pl.BlockSpec((heads, capacity, capacity), lambda h, info: (0, 0, 0), pipeline_mode=once),
                pl.BlockSpec((capacity, width), lambda h, info: (0, 0), pipeline_mode=once),
                pl.BlockSpec((capacity, width), lambda h, info: (0, 0), pipeline_mode=once),
                pl.BlockSpec(memory_space=pl.ANY),
                pl.BlockSpec(memory_space=pl.ANY),
            ],
            out_specs=[pl.BlockSpec(shape, lambda h, info: (0,) * len(shape))] * outs,
            scratch_shapes=[
                pltpu.VMEM((capacity, 3 * width), BF16),
                pltpu.VMEM((capacity, model_cols), BF16),
                pltpu.VMEM((model_cols, 3 * width), BF16),
                pltpu.SemaphoreType.DMA((6,)),
            ],
        ),
        compiler_params=pltpu.CompilerParams(vmem_limit_bytes=20 * MIB),
        cost_estimate=SMALL,
        name="attend",
    )(info, saved, saved, probs, mixed, d_attn, weight, other)


def norm_kernel(pair, offsets, home, info, mods, tokens, d_output, upper, *rest):
    blocks, rest = rest[: len(offsets)], rest[len(offsets) :]
    d_norm = rest[-1]
    width = blocks[0].shape[1] // 2
    for offset, block in zip(offsets, blocks):
        owner = info[1] ^ offset
        for part in range(2):
            start = pl.multiple_of((owner ^ (part * pair)) * width, width)
            d_norm[:, pl.ds(start, width)] = block[:, part * width : (part + 1) * width].astype(F32)
    values = tokens[...].astype(F32)
    center = values - jnp.mean(values, axis=1, keepdims=True)
    inverse = lax.rsqrt(jnp.mean(center * center, axis=1, keepdims=True) + 1e-06)
    normed = center * inverse
    gained = d_norm[...] * (1.0 + mods[0:1])
    layer = inverse * (
        gained
        - jnp.mean(gained, axis=1, keepdims=True)
        - normed * jnp.mean(gained * normed, axis=1, keepdims=True)
    )
    d_input = (d_output[...].astype(F32) + layer).astype(BF16)
    if len(rest) == 2:
        rest[0][...] = jnp.where(info[2] == home, d_input, upper[...])
    else:
        next_mods, out, d_branch = rest[:3]
        out[...] = d_input
        gated = (next_mods[1:2] * d_input.astype(F32)).astype(BF16)
        d_branch[...] = jnp.where(info[2] == home, gated, upper[...])


def norm_call(info, pair, offsets, home, mods, tokens, d_output, upper, blocks, next_mods=()):
    rows, width = tokens.shape
    tile = 32
    block_width = blocks[0].shape[1]
    row_spec = lambda cols: pl.BlockSpec((tile, cols), lambda t, info: (t, 0))
    mods_spec = pl.BlockSpec(mods.shape, lambda t, info: (0, 0))
    outs = 1 + len(next_mods)
    return pl.pallas_call(
        functools.partial(norm_kernel, pair, offsets, home),
        out_shape=[jax.ShapeDtypeStruct((rows, width), BF16)] * outs,
        grid_spec=pltpu.PrefetchScalarGridSpec(
            num_scalar_prefetch=1,
            grid=(rows // tile,),
            in_specs=[mods_spec, row_spec(width), row_spec(width), row_spec(width)]
            + [row_spec(block_width)] * len(blocks)
            + [mods_spec] * len(next_mods),
            out_specs=[row_spec(width)] * outs,
            scratch_shapes=[pltpu.VMEM((tile, width), F32)],
        ),
        compiler_params=pltpu.CompilerParams(vmem_limit_bytes=20 * MIB),
        cost_estimate=SMALL,
        name="norm",
    )(info, mods, tokens, d_output, upper, *blocks, *next_mods)


def outer_kernel(sections, slots, count, info, *refs):
    out, joined = refs[-2], refs[-1]
    refs = iter(refs[:-2])
    rows = joined.shape[1] // count

    def chosen(options):
        value = options[0][...]
        for section in range(1, sections):
            value = jnp.where(info[2] == section, options[section][...], value)
        return value

    def take(amount):
        return [next(refs) for _ in range(amount)]

    total = None
    for slot in range(slots):
        mixed = take(1)[0][...] if slot == 0 else chosen(take(sections))
        for r in range(count):
            start = pl.multiple_of((info[0] ^ r) * rows, rows)
            single = r == 0 or slot > 0
            joined[slot, pl.ds(start, rows), :] = (
                take(1)[0][...] if single else chosen(take(sections))
            )
        term = dot_tn(mixed, joined[slot])
        total = term if total is None else total + term
    out[...] = total.astype(BF16)


def outer_call(part, pair, info, own_mixed, other_mixed, own_rows, other_rows, block_cols):
    capacity, width = own_mixed.shape
    count = len(own_rows)
    rows = capacity // count
    tile = block_cols
    per_block = block_cols // tile
    mixed_spec = pl.BlockSpec((capacity, width), lambda t, info: (0, 0))

    def own_map(t, info):
        return (0, (info[1] ^ (part * pair)) * per_block + t)

    def other_map(t, info):
        return (0, part * per_block + t)

    operands, specs = [own_mixed], [mixed_spec]
    for options in own_rows:
        operands += options
        specs += [pl.BlockSpec((rows, tile), own_map)] * len(options)
    for mixed, blocks in zip(other_mixed, other_rows):
        operands += mixed + blocks
        specs += [mixed_spec] * len(mixed) + [pl.BlockSpec((rows, tile), other_map)] * len(blocks)
    return pl.pallas_call(
        functools.partial(outer_kernel, len(own_rows[1]), 1 + len(other_mixed), count),
        out_shape=jax.ShapeDtypeStruct((width, block_cols), BF16),
        grid_spec=pltpu.PrefetchScalarGridSpec(
            num_scalar_prefetch=1,
            grid=(per_block,),
            in_specs=specs,
            out_specs=pl.BlockSpec((width, tile), lambda t, info: (0, t)),
            scratch_shapes=[pltpu.VMEM((1 + len(other_mixed), capacity, tile), BF16)],
        ),
        compiler_params=pltpu.CompilerParams(vmem_limit_bytes=24 * MIB),
        cost_estimate=SMALL,
        name="outer",
    )(info, *operands)


def after(value, *tokens):
    return lax.optimization_barrier((value, *tokens))[0]


def body(section_input, saved_qkv, modulation, w_qkv, w_out, lengths, student_out, teacher_target):
    section_total = lax.axis_size("section")
    seq_total = lax.axis_size("seq")
    dp_total = lax.axis_size("dp")
    section_pos = lax.axis_index("section")
    seq_pos = lax.axis_index("seq")
    dp_pos = lax.axis_index("dp")
    tokens = section_input[0, 0]
    mods = modulation[0, 0]
    shard_rows, model_width = tokens.shape
    capacity = saved_qkv.shape[2]
    block_cols = model_width // dp_total
    pair = 1
    offsets = [e for e in range(dp_total) if e & pair == 0]
    saved = saved_qkv[0, 0].transpose(1, 0, 2)
    weight = w_qkv[0].transpose(1, 0, 2)
    weight_out = w_out[0]

    def flat(section, seq, dp):
        return (section * seq_total + seq) * dp_total + dp

    def moved(value, sections, target):
        pairs = [
            (flat(s, i, j), flat(*target(s, i, j)))
            for s in sections
            for i in range(seq_total)
            for j in range(dp_total)
        ]
        return lax.ppermute(value, AXES, pairs)

    def over_dp(value, offset, sections, steps_down=0):
        return moved(value, sections, lambda s, i, j: (s - steps_down, i, j ^ offset))

    def over_seq(value, offset, sections):
        return moved(value, sections, lambda s, i, j: (s, i ^ offset, j))

    def section_shift(value, section, steps):
        return moved(value, [section], lambda s, i, j: (s + steps, i, j))

    info = jnp.stack([seq_pos, dp_pos, section_pos]).astype(jnp.int32)
    positions = seq_pos * shard_rows + jnp.arange(shard_rows, dtype=jnp.int32)
    gap = student_out[0].astype(F32) - teacher_target[0].astype(F32)
    loss_grad = jnp.where((positions < lengths[0])[:, None], gap, 0.0).astype(BF16)

    def prefetch(section, saved, weight):
        others = [over_dp(saved, e, [section]) for e in offsets[1:]]
        return others, over_dp(weight, pair, [section])

    def halved(kept, sent, sections, token):
        offset = 1
        while True:
            total = kept.astype(F32) + over_seq(sent, offset, sections).astype(F32)
            if total.shape[0] == 1:
                return total[0].astype(BF16)
            offset *= 2
            kept, sent = total[0::2], after(total[1::2].astype(BF16), token)

    def column_pair(rows, owner):
        first = lax.dynamic_slice_in_dim(rows, owner * block_cols, block_cols, 1)
        second = lax.dynamic_slice_in_dim(rows, (owner ^ 1) * block_cols, block_cols, 1)
        return jnp.concatenate([first, second], axis=1)

    def slots_of(saved_others):
        saved_slots = [saved_sent] + saved_others
        probs_slots = [own_probs] + [
            probs_call(info, saved_slots[k], capacity) for k in range(1, len(saved_slots))
        ]
        return saved_slots, probs_slots

    top = section_total - 1
    d_output = loss_grad
    d_branch = (mods[1] * d_output.astype(F32)).astype(BF16)
    high, low = lengths[0] // 256, lengths[0] % 256
    tail = jnp.zeros((3, TAIL, saved.shape[2]), BF16)
    tail = tail.at[0, 0, 0].set((high).astype(BF16))
    tail = tail.at[0, 0, 1].set((low).astype(BF16))
    saved_sent = jnp.concatenate([saved, tail], axis=1)
    prefetched = prefetch(top, saved_sent, weight)
    own_probs = probs_call(info, saved_sent, capacity)
    grad_up, uppers = None, []
    held = (own_probs[1],)
    every = list(range(section_total))
    rows_of, mixed_of = [None] * section_total, [None] * section_total
    for section in reversed(every):
        only = [section]
        saved_others, weight_other = prefetched
        own_rows = [d_branch] + [over_seq(d_branch, r, only) for r in range(1, seq_total)]
        if section < top:
            saved_slots, probs_slots = slots_of(saved_others)
            held = held + (weight_other, probs_slots[-1][1])
        ready_rows = own_rows[:-1] + [after(own_rows[-1], *held)] if held else own_rows
        d_attn = d_attn_call(info, ready_rows, weight_out)
        if section == top:
            saved_slots, probs_slots = slots_of(saved_others)
        leaving = d_attn
        if section == 0:
            all_columns = [
                over_dp(column_pair(d_branch, dp_pos ^ e), e, every) for e in offsets[1:]
            ]
        d_attns = [d_attn] + [over_dp(leaving, e, only) for e in offsets[1:]]
        rows_of[section] = own_rows
        mixed_of[section] = [mixed for _, mixed in probs_slots[1:]]

        waits = ()
        all_parts = {}
        for k in range(len(offsets)):
            probs, mixed = probs_slots[k]
            if k == 1 and section > 0:
                ready = [mixed for _, mixed in probs_slots[1:]]
                next_mods = section_shift(after(mods, *waits, *ready, *d_attns[1:]), section, -1)
                next_saved = [
                    over_dp(after(saved_sent, next_mods), e, [section - 1]) for e in offsets[1:]
                ]
                waits = waits + (next_mods,)
            all_parts[k] = attend_call(
                info,
                saved_slots[k],
                probs,
                mixed,
                after(d_attns[k], *waits) if waits else d_attns[k],
                weight,
                weight_other,
                seq_total,
                k == 0,
                section,
            )
            waits = (all_parts[k][0],)
        if section > 0:
            next_other = over_dp(after(weight, *waits), pair, [section - 1])
            next_tokens = section_shift(after(tokens, *waits), section, -1)
        down = 1 if section > 0 else 0
        home = [None] * len(offsets)
        for k in reversed(range(len(offsets))):
            parts = all_parts[k]
            if k == 0:
                ready = [mixed for _, mixed in probs_slots[1:]] + d_attns[1:]
                total = halved(parts[0], after(parts[1], *ready), only, total)
            else:
                total = parts[0].astype(F32)
                for r in range(1, seq_total):
                    total = total + over_seq(parts[r], r, only).astype(F32)
                total = total.astype(BF16)
            e = offsets[k]
            home[k] = over_dp(total, e, only, down) if e or down else total

        if section > 0:
            prefetched = next_saved, next_other
            d_output, d_branch = norm_call(
                info,
                pair,
                offsets,
                section - 1,
                next_mods,
                next_tokens,
                d_output,
                d_branch,
                home,
                (mods,),
            )
            uppers.append((section, d_output))
            held = ()
    for section, d_input in uppers:
        back = section_shift(after(d_input, *waits), section - 1, 1)
        grad_up = back if grad_up is None else jnp.where(section_pos == section, back, grad_up)
    (grad_in,) = norm_call(info, pair, offsets, 0, mods, tokens, d_output, grad_up, home)

    other_rows = [
        [columns] + [over_seq(columns, r, every) for r in range(1, seq_total)]
        for columns in all_columns
    ]
    row_options = [[rows_of[s][r] for s in every] for r in range(1, seq_total)]
    mixed_options = [[mixed_of[s][k] for s in every] for k in range(len(offsets) - 1)]

    def outer_part(part, *tokens):
        own_options = [[after(d_branch, *tokens)]] + row_options
        return outer_call(
            part, pair, info, own_probs[1], mixed_options, own_options, other_rows, block_cols
        )

    received = over_dp(outer_part(1, *waits), pair, every)
    kept = outer_part(0, received)
    grad_out = (kept.astype(F32) + received.astype(F32)).astype(BF16)
    return grad_in[None, None], grad_out[None]


def solution(mesh):
    in_specs = (
        P("section", "dp", "seq", None),
        P("section", "dp", None, None, "seq"),
        P("section", "dp", None, None),
        P("section", "dp", None, "seq"),
        P("section", "seq", None),
        P("dp"),
        P("dp", "seq", None),
        P("dp", "seq", None),
    )
    out_specs = (P("section", "dp", "seq", None), P("section", "seq", "dp"))
    return jax.shard_map(body, mesh=mesh, in_specs=in_specs, out_specs=out_specs, check_vma=False)
```

```python
import functools
import math

import jax
import jax.numpy as jnp
from jax import lax
from jax.experimental import pallas as pl
from jax.experimental.pallas import tpu as pltpu
from jax.sharding import PartitionSpec as P

HEAD_DIM = 128
AXES = ("section", "seq", "dp")
F32 = jnp.float32
BF16 = jnp.bfloat16
MIB = 1024 * 1024
TAIL = 16
SMALL = pl.CostEstimate(flops=1024, bytes_accessed=1024, transcendentals=0)


def dot_nt(left, right):
    return lax.dot_general(left, right, (((1,), (1,)), ((), ())), preferred_element_type=F32)


def dot_nn(left, right):
    return lax.dot_general(left, right, (((1,), (0,)), ((), ())), preferred_element_type=F32)


def dot_tn(left, right):
    return lax.dot_general(left, right, (((0,), (0,)), ((), ())), preferred_element_type=F32)


def d_attn_kernel(info, *refs):
    blocks, w_out, out, joined, total = refs[:-4], refs[-4], refs[-3], refs[-2], refs[-1]
    rows = blocks[0].shape[0]
    step = pl.program_id(0)
    for r, block in enumerate(blocks):
        start = pl.multiple_of((info[0] ^ r) * rows, rows)
        joined[pl.ds(start, rows), :] = block[...]
    term = dot_nt(joined[...], w_out[...])

    @pl.when(step == 0)
    def _():
        total[...] = term

    @pl.when(step > 0)
    def _():
        total[...] += term

    @pl.when(step == pl.num_programs(0) - 1)
    def _():
        out[...] = total[...].astype(BF16)


def d_attn_call(info, blocks, w_out):
    rows, width = blocks[0].shape
    heads_width = w_out.shape[0]
    count = len(blocks)
    tile = width // 4
    return pl.pallas_call(
        d_attn_kernel,
        out_shape=jax.ShapeDtypeStruct((rows * count, heads_width), BF16),
        grid_spec=pltpu.PrefetchScalarGridSpec(
            num_scalar_prefetch=1,
            grid=(width // tile,),
            in_specs=[pl.BlockSpec((rows, tile), lambda t, info: (0, t))] * count
            + [pl.BlockSpec((heads_width, tile), lambda t, info: (0, t))],
            out_specs=pl.BlockSpec((rows * count, heads_width), lambda t, info: (0, 0)),
            scratch_shapes=[
                pltpu.VMEM((rows * count, tile), BF16),
                pltpu.VMEM((rows * count, heads_width), F32),
            ],
        ),
        compiler_params=pltpu.CompilerParams(vmem_limit_bytes=16 * MIB),
        cost_estimate=SMALL,
        name="d_attn",
    )(info, *blocks, w_out)


def live_count(tail):
    row = tail[0, 0:1, :].astype(F32)
    lane = lax.broadcasted_iota(jnp.int32, row.shape, 1)
    return jnp.sum(row * jnp.where(lane == 0, 256.0, 1.0)).astype(jnp.int32)


def tail_spec(capacity):
    return pl.BlockSpec((1, TAIL, HEAD_DIM), lambda h, info: (0, capacity // TAIL, 0))


def probs_kernel(info, saved, tail, probs, mixed):
    capacity = mixed.shape[0]
    live = live_count(tail)
    factor = 1.0 / math.sqrt(HEAD_DIM)

    def one_head(size):
        queries, keys, values = saved[0, :size], saved[1, :size], saved[2, :size]
        scores = dot_nt(keys, queries) * factor
        alive = lax.broadcasted_iota(jnp.int32, (size, 1), 0) < live
        scores = jnp.where(alive, scores, -1e30)
        weights = jnp.exp(scores - jnp.max(scores, axis=0, keepdims=True))
        weights = weights * (1.0 / jnp.sum(weights, axis=0, keepdims=True))
        rounded = weights.astype(BF16)
        probs[0, :size, :size] = rounded
        mixed[:size] = dot_tn(rounded, values).astype(BF16)
        if size < capacity:
            mixed[size:] = jnp.zeros((capacity - size, HEAD_DIM), BF16)

    half = capacity // 2

    @pl.when(live > half)
    def _():
        one_head(capacity)

    @pl.when(live <= half)
    def _():
        one_head(half)


def probs_call(info, saved, capacity):
    width = saved.shape[2]
    heads = width // HEAD_DIM
    return pl.pallas_call(
        probs_kernel,
        out_shape=[
            jax.ShapeDtypeStruct((heads, capacity, capacity), BF16),
            jax.ShapeDtypeStruct((capacity, width), BF16),
        ],
        grid_spec=pltpu.PrefetchScalarGridSpec(
            num_scalar_prefetch=1,
            grid=(heads,),
            in_specs=[
                pl.BlockSpec((3, capacity, HEAD_DIM), lambda h, info: (0, 0, h)),
                tail_spec(capacity),
            ],
            out_specs=[
                pl.BlockSpec((1, capacity, capacity), lambda h, info: (h, 0, 0)),
                pl.BlockSpec((capacity, HEAD_DIM), lambda h, info: (0, h)),
            ],
        ),
        compiler_params=pltpu.CompilerParams(vmem_limit_bytes=16 * MIB),
        cost_estimate=SMALL,
        name="probs",
    )(info, saved, saved)


def attend_kernel(section, info, saved, tail, probs, mixed, d_attn, weight, other, *rest):
    outs, (grads, partial, w_vmem, w_sem) = rest[:-4], rest[-4:]
    rows = outs[0].shape[-2]
    capacity = d_attn.shape[0]
    count = capacity // rows
    grouped = len(outs) < count
    block = weight.shape[1]
    width = grads.shape[1] // 3
    heads = width // HEAD_DIM
    me, live, active = info[0], live_count(tail), info[2] == section
    factor = 1.0 / math.sqrt(HEAD_DIM)
    copies = [
        pltpu.make_async_copy(
            source.at[part],
            w_vmem.at[pl.ds(side * block, block), pl.ds(part * width, width)],
            w_sem.at[3 * side + part],
        )
        for side, source in enumerate((weight, other))
        for part in range(3)
    ]

    @pl.when(active)
    def _():
        for copy in copies:
            copy.start()

    def all_heads(size):
        for head in range(heads):
            one_head(size, head)

    def one_head(size, head):
        lanes = slice(head * HEAD_DIM, (head + 1) * HEAD_DIM)

        def columns(part):
            first = part * width + head * HEAD_DIM
            return slice(first, first + HEAD_DIM)

        queries, keys, values = saved[0, :size, lanes], saved[1, :size, lanes], saved[2, :size, lanes]
        upstream = d_attn[:size, lanes]
        weights = probs[head, :size, :size]
        product = upstream.astype(F32) * mixed[:size, lanes].astype(F32)
        delta = jnp.sum(product.T, axis=0, keepdims=True)
        d_weights = dot_nt(values, upstream)
        d_scores = (weights.astype(F32) * (d_weights - delta) * factor).astype(BF16)
        grads[:size, columns(0)] = dot_nn(keys.T, d_scores).T.astype(BF16)
        grads[:size, columns(1)] = dot_nn(d_scores, queries).astype(BF16)
        grads[:size, columns(2)] = dot_nn(weights, upstream).astype(BF16)

    half = capacity // 2

    @pl.when(active & (live > half))
    def _():
        all_heads(capacity)

    @pl.when(active & (live <= half))
    def _():
        all_heads(half)

    @pl.when(active)
    def _():
        for copy in copies:
            copy.wait()
        step = min(512, 2 * block)

        def project(size):
            for first in range(0, 2 * block, step):
                product = dot_nt(grads[:size], w_vmem[first : first + step])
                partial[:size, first : first + step] = product.astype(BF16)
            if size < capacity:
                partial[size:] = jnp.zeros((capacity - size, 2 * block), BF16)
            for r in range(count):
                start = pl.multiple_of((me ^ r) * rows, rows)
                block_rows = partial[pl.ds(start, rows)]
                if grouped:
                    outs[r % 2][r // 2] = block_rows
                else:
                    outs[r][...] = block_rows

        @pl.when(live > half)
        def _():
            project(capacity)

        @pl.when(live <= half)
        def _():
            project(half)


def attend_call(info, saved, probs, mixed, d_attn, weight, other, count, grouped, section):
    capacity, width = d_attn.shape
    rows = capacity // count
    model_cols = 2 * weight.shape[1]
    heads = width // HEAD_DIM
    if grouped:
        outs, shape = 2, (count // 2, rows, model_cols)
    else:
        outs, shape = count, (rows, model_cols)
    once = pl.Buffered(1)
    return pl.pallas_call(
        functools.partial(attend_kernel, section),
        out_shape=[jax.ShapeDtypeStruct(shape, BF16)] * outs,
        grid_spec=pltpu.PrefetchScalarGridSpec(
            num_scalar_prefetch=1,
            grid=(1,),
            in_specs=[
                pl.BlockSpec((3, capacity, width), lambda h, info: (0, 0, 0), pipeline_mode=once),
                tail_spec(capacity),
                pl.BlockSpec((heads, capacity, capacity), lambda h, info: (0, 0, 0), pipeline_mode=once),
                pl.BlockSpec((capacity, width), lambda h, info: (0, 0), pipeline_mode=once),
                pl.BlockSpec((capacity, width), lambda h, info: (0, 0), pipeline_mode=once),
                pl.BlockSpec(memory_space=pl.ANY),
                pl.BlockSpec(memory_space=pl.ANY),
            ],
            out_specs=[pl.BlockSpec(shape, lambda h, info: (0,) * len(shape))] * outs,
            scratch_shapes=[
                pltpu.VMEM((capacity, 3 * width), BF16),
                pltpu.VMEM((capacity, model_cols), BF16),
                pltpu.VMEM((model_cols, 3 * width), BF16),
                pltpu.SemaphoreType.DMA((6,)),
            ],
        ),
        compiler_params=pltpu.CompilerParams(vmem_limit_bytes=20 * MIB),
        cost_estimate=SMALL,
        name="attend",
    )(info, saved, saved, probs, mixed, d_attn, weight, other)


def norm_kernel(pair, offsets, home, info, mods, tokens, d_output, upper, *rest):
    blocks, rest = rest[: len(offsets)], rest[len(offsets) :]
    d_norm = rest[-1]
    width = blocks[0].shape[1] // 2
    for offset, block in zip(offsets, blocks):
        owner = info[1] ^ offset
        for part in range(2):
            start = pl.multiple_of((owner ^ (part * pair)) * width, width)
            d_norm[:, pl.ds(start, width)] = block[:, part * width : (part + 1) * width].astype(F32)
    values = tokens[...].astype(F32)
    center = values - jnp.mean(values, axis=1, keepdims=True)
    inverse = lax.rsqrt(jnp.mean(center * center, axis=1, keepdims=True) + 1e-06)
    normed = center * inverse
    gained = d_norm[...] * (1.0 + mods[0:1])
    layer = inverse * (
        gained
        - jnp.mean(gained, axis=1, keepdims=True)
        - normed * jnp.mean(gained * normed, axis=1, keepdims=True)
    )
    d_input = (d_output[...].astype(F32) + layer).astype(BF16)
    if len(rest) == 2:
        rest[0][...] = jnp.where(info[2] == home, d_input, upper[...])
    else:
        next_mods, out, d_branch = rest[:3]
        out[...] = d_input
        gated = (next_mods[1:2] * d_input.astype(F32)).astype(BF16)
        d_branch[...] = jnp.where(info[2] == home, gated, upper[...])


def norm_call(info, pair, offsets, home, mods, tokens, d_output, upper, blocks, next_mods=()):
    rows, width = tokens.shape
    tile = 64
    block_width = blocks[0].shape[1]
    row_spec = lambda cols: pl.BlockSpec((tile, cols), lambda t, info: (t, 0))
    mods_spec = pl.BlockSpec(mods.shape, lambda t, info: (0, 0))
    outs = 1 + len(next_mods)
    return pl.pallas_call(
        functools.partial(norm_kernel, pair, offsets, home),
        out_shape=[jax.ShapeDtypeStruct((rows, width), BF16)] * outs,
        grid_spec=pltpu.PrefetchScalarGridSpec(
            num_scalar_prefetch=1,
            grid=(rows // tile,),
            in_specs=[mods_spec, row_spec(width), row_spec(width), row_spec(width)]
            + [row_spec(block_width)] * len(blocks)
            + [mods_spec] * len(next_mods),
            out_specs=[row_spec(width)] * outs,
            scratch_shapes=[pltpu.VMEM((tile, width), F32)],
        ),
        compiler_params=pltpu.CompilerParams(vmem_limit_bytes=20 * MIB),
        cost_estimate=SMALL,
        name="norm",
    )(info, mods, tokens, d_output, upper, *blocks, *next_mods)


def outer_kernel(sections, slots, count, info, *refs):
    out, joined = refs[-2], refs[-1]
    refs = iter(refs[:-2])
    rows = joined.shape[1] // count

    def chosen(options):
        value = options[0][...]
        for section in range(1, sections):
            value = jnp.where(info[2] == section, options[section][...], value)
        return value

    def take(amount):
        return [next(refs) for _ in range(amount)]

    total = None
    for slot in range(slots):
        mixed = take(1)[0][...] if slot == 0 else chosen(take(sections))
        for r in range(count):
            start = pl.multiple_of((info[0] ^ r) * rows, rows)
            single = r == 0 or slot > 0
            joined[slot, pl.ds(start, rows), :] = (
                take(1)[0][...] if single else chosen(take(sections))
            )
        term = dot_tn(mixed, joined[slot])
        total = term if total is None else total + term
    out[...] = total.astype(BF16)


def outer_call(part, pair, info, own_mixed, other_mixed, own_rows, other_rows, block_cols):
    capacity, width = own_mixed.shape
    count = len(own_rows)
    rows = capacity // count
    tile = block_cols
    per_block = block_cols // tile
    mixed_spec = pl.BlockSpec((capacity, width), lambda t, info: (0, 0))

    def own_map(t, info):
        return (0, (info[1] ^ (part * pair)) * per_block + t)

    def other_map(t, info):
        return (0, part * per_block + t)

    operands, specs = [own_mixed], [mixed_spec]
    for options in own_rows:
        operands += options
        specs += [pl.BlockSpec((rows, tile), own_map)] * len(options)
    for mixed, blocks in zip(other_mixed, other_rows):
        operands += mixed + blocks
        specs += [mixed_spec] * len(mixed) + [pl.BlockSpec((rows, tile), other_map)] * len(blocks)
    return pl.pallas_call(
        functools.partial(outer_kernel, len(own_rows[1]), 1 + len(other_mixed), count),
        out_shape=jax.ShapeDtypeStruct((width, block_cols), BF16),
        grid_spec=pltpu.PrefetchScalarGridSpec(
            num_scalar_prefetch=1,
            grid=(per_block,),
            in_specs=specs,
            out_specs=pl.BlockSpec((width, tile), lambda t, info: (0, t)),
            scratch_shapes=[pltpu.VMEM((1 + len(other_mixed), capacity, tile), BF16)],
        ),
        compiler_params=pltpu.CompilerParams(vmem_limit_bytes=24 * MIB),
        cost_estimate=SMALL,
        name="outer",
    )(info, *operands)


def after(value, *tokens):
    return lax.optimization_barrier((value, *tokens))[0]


def body(section_input, saved_qkv, modulation, w_qkv, w_out, lengths, student_out, teacher_target):
    section_total = lax.axis_size("section")
    seq_total = lax.axis_size("seq")
    dp_total = lax.axis_size("dp")
    section_pos = lax.axis_index("section")
    seq_pos = lax.axis_index("seq")
    dp_pos = lax.axis_index("dp")
    tokens = section_input[0, 0]
    mods = modulation[0, 0]
    shard_rows, model_width = tokens.shape
    capacity = saved_qkv.shape[2]
    block_cols = model_width // dp_total
    pair = 1
    offsets = [e for e in range(dp_total) if e & pair == 0]
    saved = saved_qkv[0, 0].transpose(1, 0, 2)
    weight = w_qkv[0].transpose(1, 0, 2)
    weight_out = w_out[0]

    def flat(section, seq, dp):
        return (section * seq_total + seq) * dp_total + dp

    def moved(value, sections, target):
        pairs = [
            (flat(s, i, j), flat(*target(s, i, j)))
            for s in sections
            for i in range(seq_total)
            for j in range(dp_total)
        ]
        return lax.ppermute(value, AXES, pairs)

    def over_dp(value, offset, sections, steps_down=0):
        return moved(value, sections, lambda s, i, j: (s - steps_down, i, j ^ offset))

    def over_seq(value, offset, sections):
        return moved(value, sections, lambda s, i, j: (s, i ^ offset, j))

    def section_shift(value, section, steps):
        return moved(value, [section], lambda s, i, j: (s + steps, i, j))

    info = jnp.stack([seq_pos, dp_pos, section_pos]).astype(jnp.int32)
    positions = seq_pos * shard_rows + jnp.arange(shard_rows, dtype=jnp.int32)
    gap = student_out[0].astype(F32) - teacher_target[0].astype(F32)
    loss_grad = jnp.where((positions < lengths[0])[:, None], gap, 0.0).astype(BF16)

    def prefetch(section, saved, weight):
        others = [over_dp(saved, e, [section]) for e in offsets[1:]]
        return others, over_dp(weight, pair, [section])

    def halved(kept, sent, sections, token):
        offset = 1
        while True:
            total = kept.astype(F32) + over_seq(sent, offset, sections).astype(F32)
            if total.shape[0] == 1:
                return total[0].astype(BF16)
            offset *= 2
            kept, sent = total[0::2], after(total[1::2].astype(BF16), token)

    def column_pair(rows, owner):
        first = lax.dynamic_slice_in_dim(rows, owner * block_cols, block_cols, 1)
        second = lax.dynamic_slice_in_dim(rows, (owner ^ 1) * block_cols, block_cols, 1)
        return jnp.concatenate([first, second], axis=1)

    def slots_of(saved_others):
        saved_slots = [saved_sent] + saved_others
        probs_slots = [own_probs] + [
            probs_call(info, saved_slots[k], capacity) for k in range(1, len(saved_slots))
        ]
        return saved_slots, probs_slots

    top = section_total - 1
    d_output = loss_grad
    d_branch = (mods[1] * d_output.astype(F32)).astype(BF16)
    high, low = lengths[0] // 256, lengths[0] % 256
    tail = jnp.zeros((3, TAIL, saved.shape[2]), BF16)
    tail = tail.at[0, 0, 0].set((high).astype(BF16))
    tail = tail.at[0, 0, 1].set((low).astype(BF16))
    saved_sent = jnp.concatenate([saved, tail], axis=1)
    prefetched = prefetch(top, saved_sent, weight)
    own_probs = probs_call(info, saved_sent, capacity)
    grad_up, uppers = None, []
    held = (own_probs[1],)
    every = list(range(section_total))
    rows_of, mixed_of = [None] * section_total, [None] * section_total
    for section in reversed(every):
        only = [section]
        saved_others, weight_other = prefetched
        own_rows = [d_branch] + [over_seq(d_branch, r, only) for r in range(1, seq_total)]
        if section < top:
            saved_slots, probs_slots = slots_of(saved_others)
            held = held + (weight_other, probs_slots[-1][1])
        ready_rows = own_rows[:-1] + [after(own_rows[-1], *held)] if held else own_rows
        d_attn = d_attn_call(info, ready_rows, weight_out)
        if section == top:
            saved_slots, probs_slots = slots_of(saved_others)
        leaving = d_attn
        if section == 0:
            all_columns = [
                over_dp(column_pair(d_branch, dp_pos ^ e), e, every) for e in offsets[1:]
            ]
        d_attns = [d_attn] + [over_dp(leaving, e, only) for e in offsets[1:]]
        rows_of[section] = own_rows
        mixed_of[section] = [mixed for _, mixed in probs_slots[1:]]

        waits = ()
        all_parts = {}
        for k in range(len(offsets)):
            probs, mixed = probs_slots[k]
            if k == 1 and section > 0:
                ready = [mixed for _, mixed in probs_slots[1:]]
                next_mods = section_shift(after(mods, *waits, *ready, *d_attns[1:]), section, -1)
                next_saved = [
                    over_dp(after(saved_sent, next_mods), e, [section - 1]) for e in offsets[1:]
                ]
                waits = waits + (next_mods,)
            all_parts[k] = attend_call(
                info,
                saved_slots[k],
                probs,
                mixed,
                after(d_attns[k], *waits) if waits else d_attns[k],
                weight,
                weight_other,
                seq_total,
                k == 0,
                section,
            )
            waits = (all_parts[k][0],)
        if section > 0:
            next_other = over_dp(after(weight, *waits), pair, [section - 1])
            next_tokens = section_shift(after(tokens, probs_slots[-1][1]), section, -1)
        down = 1 if section > 0 else 0
        home = [None] * len(offsets)
        for k in reversed(range(len(offsets))):
            parts = all_parts[k]
            if k == 0:
                ready = [mixed for _, mixed in probs_slots[1:]] + d_attns[1:]
                late = waits[0] if section == top else total
                total = halved(parts[0], after(parts[1], *ready), only, late)
            else:
                total = parts[0].astype(F32)
                for r in range(1, seq_total):
                    total = total + over_seq(parts[r], r, only).astype(F32)
                total = total.astype(BF16)
            e = offsets[k]
            home[k] = over_dp(total, e, only, down) if e or down else total

        if section > 0:
            prefetched = next_saved, next_other
            d_output, d_branch = norm_call(
                info,
                pair,
                offsets,
                section - 1,
                next_mods,
                next_tokens,
                d_output,
                d_branch,
                home,
                (mods,),
            )
            uppers.append((section, d_output))
            held = ()
    for section, d_input in uppers:
        back = section_shift(after(d_input, *waits), section - 1, 1)
        grad_up = back if grad_up is None else jnp.where(section_pos == section, back, grad_up)
    (grad_in,) = norm_call(info, pair, offsets, 0, mods, tokens, d_output, grad_up, home)

    other_rows = [
        [columns] + [over_seq(columns, r, every) for r in range(1, seq_total)]
        for columns in all_columns
    ]
    row_options = [[rows_of[s][r] for s in every] for r in range(1, seq_total)]
    mixed_options = [[mixed_of[s][k] for s in every] for k in range(len(offsets) - 1)]

    def outer_part(part, *tokens):
        own_options = [[after(d_branch, *tokens)]] + row_options
        return outer_call(
            part, pair, info, own_probs[1], mixed_options, own_options, other_rows, block_cols
        )

    received = over_dp(outer_part(1, *waits), pair, every)
    kept = outer_part(0, received)
    grad_out = (kept.astype(F32) + received.astype(F32)).astype(BF16)
    return grad_in[None, None], grad_out[None]


def solution(mesh):
    in_specs = (
        P("section", "dp", "seq", None),
        P("section", "dp", None, None, "seq"),
        P("section", "dp", None, None),
        P("section", "dp", None, "seq"),
        P("section", "seq", None),
        P("dp"),
        P("dp", "seq", None),
        P("dp", "seq", None),
    )
    out_specs = (P("section", "dp", "seq", None), P("section", "seq", "dp"))
    return jax.shard_map(body, mesh=mesh, in_specs=in_specs, out_specs=out_specs, check_vma=False)
```

```python
import functools
import math

import jax
import jax.numpy as jnp
from jax import lax
from jax.experimental import pallas as pl
from jax.experimental.pallas import tpu as pltpu
from jax.sharding import PartitionSpec as P

HEAD_DIM = 128
AXES = ("section", "seq", "dp")
F32 = jnp.float32
BF16 = jnp.bfloat16
MIB = 1024 * 1024
TAIL = 16
SMALL = pl.CostEstimate(flops=1024, bytes_accessed=1024, transcendentals=0)


def dot_nt(left, right):
    return lax.dot_general(left, right, (((1,), (1,)), ((), ())), preferred_element_type=F32)


def dot_nn(left, right):
    return lax.dot_general(left, right, (((1,), (0,)), ((), ())), preferred_element_type=F32)


def dot_tn(left, right):
    return lax.dot_general(left, right, (((0,), (0,)), ((), ())), preferred_element_type=F32)


def d_attn_kernel(info, *refs):
    blocks, w_out, out, joined, total = refs[:-4], refs[-4], refs[-3], refs[-2], refs[-1]
    rows = blocks[0].shape[0]
    step = pl.program_id(0)
    for r, block in enumerate(blocks):
        start = pl.multiple_of((info[0] ^ r) * rows, rows)
        joined[pl.ds(start, rows), :] = block[...]
    term = dot_nt(joined[...], w_out[...])

    @pl.when(step == 0)
    def _():
        total[...] = term

    @pl.when(step > 0)
    def _():
        total[...] += term

    @pl.when(step == pl.num_programs(0) - 1)
    def _():
        out[...] = total[...].astype(BF16)


def d_attn_call(info, blocks, w_out):
    rows, width = blocks[0].shape
    heads_width = w_out.shape[0]
    count = len(blocks)
    tile = width // 4
    return pl.pallas_call(
        d_attn_kernel,
        out_shape=jax.ShapeDtypeStruct((rows * count, heads_width), BF16),
        grid_spec=pltpu.PrefetchScalarGridSpec(
            num_scalar_prefetch=1,
            grid=(width // tile,),
            in_specs=[pl.BlockSpec((rows, tile), lambda t, info: (0, t))] * count
            + [pl.BlockSpec((heads_width, tile), lambda t, info: (0, t))],
            out_specs=pl.BlockSpec((rows * count, heads_width), lambda t, info: (0, 0)),
            scratch_shapes=[
                pltpu.VMEM((rows * count, tile), BF16),
                pltpu.VMEM((rows * count, heads_width), F32),
            ],
        ),
        compiler_params=pltpu.CompilerParams(vmem_limit_bytes=16 * MIB),
        cost_estimate=SMALL,
        name="d_attn",
    )(info, *blocks, w_out)


def live_count(tail):
    row = tail[0, 0:1, :].astype(F32)
    lane = lax.broadcasted_iota(jnp.int32, row.shape, 1)
    return jnp.sum(row * jnp.where(lane == 0, 256.0, 1.0)).astype(jnp.int32)


def tail_spec(capacity):
    return pl.BlockSpec((1, TAIL, HEAD_DIM), lambda h, info: (0, capacity // TAIL, 0))


def probs_kernel(info, saved, tail, probs, mixed):
    capacity = mixed.shape[0]
    live = live_count(tail)
    factor = 1.0 / math.sqrt(HEAD_DIM)

    def one_head(size):
        queries, keys, values = saved[0, :size], saved[1, :size], saved[2, :size]
        scores = dot_nt(keys, queries) * factor
        alive = lax.broadcasted_iota(jnp.int32, (size, 1), 0) < live
        scores = jnp.where(alive, scores, -1e30)
        weights = jnp.exp(scores - jnp.max(scores, axis=0, keepdims=True))
        weights = weights * (1.0 / jnp.sum(weights, axis=0, keepdims=True))
        rounded = weights.astype(BF16)
        probs[0, :size, :size] = rounded
        mixed[:size] = dot_tn(rounded, values).astype(BF16)
        if size < capacity:
            mixed[size:] = jnp.zeros((capacity - size, HEAD_DIM), BF16)

    half = capacity // 2

    @pl.when(live > half)
    def _():
        one_head(capacity)

    @pl.when(live <= half)
    def _():
        one_head(half)


def probs_call(info, saved, capacity):
    width = saved.shape[2]
    heads = width // HEAD_DIM
    return pl.pallas_call(
        probs_kernel,
        out_shape=[
            jax.ShapeDtypeStruct((heads, capacity, capacity), BF16),
            jax.ShapeDtypeStruct((capacity, width), BF16),
        ],
        grid_spec=pltpu.PrefetchScalarGridSpec(
            num_scalar_prefetch=1,
            grid=(heads,),
            in_specs=[
                pl.BlockSpec((3, capacity, HEAD_DIM), lambda h, info: (0, 0, h)),
                tail_spec(capacity),
            ],
            out_specs=[
                pl.BlockSpec((1, capacity, capacity), lambda h, info: (h, 0, 0)),
                pl.BlockSpec((capacity, HEAD_DIM), lambda h, info: (0, h)),
            ],
        ),
        compiler_params=pltpu.CompilerParams(vmem_limit_bytes=16 * MIB),
        cost_estimate=SMALL,
        name="probs",
    )(info, saved, saved)


def attend_kernel(section, info, saved, tail, probs, mixed, d_attn, weight, other, *rest):
    outs, (grads, partial, w_vmem, w_sem) = rest[:-4], rest[-4:]
    rows = outs[0].shape[-2]
    capacity = d_attn.shape[0]
    count = capacity // rows
    grouped = len(outs) < count
    block = weight.shape[1]
    width = grads.shape[1] // 3
    heads = width // HEAD_DIM
    me, live, active = info[0], live_count(tail), info[2] == section
    factor = 1.0 / math.sqrt(HEAD_DIM)
    copies = [
        pltpu.make_async_copy(
            source.at[part],
            w_vmem.at[pl.ds(side * block, block), pl.ds(part * width, width)],
            w_sem.at[3 * side + part],
        )
        for side, source in enumerate((weight, other))
        for part in range(3)
    ]

    @pl.when(active)
    def _():
        for copy in copies:
            copy.start()

    def all_heads(size):
        for head in range(heads):
            one_head(size, head)

    def one_head(size, head):
        lanes = slice(head * HEAD_DIM, (head + 1) * HEAD_DIM)

        def columns(part):
            first = part * width + head * HEAD_DIM
            return slice(first, first + HEAD_DIM)

        queries, keys, values = saved[0, :size, lanes], saved[1, :size, lanes], saved[2, :size, lanes]
        upstream = d_attn[:size, lanes]
        weights = probs[head, :size, :size]
        product = upstream.astype(F32) * mixed[:size, lanes].astype(F32)
        delta = jnp.sum(product.T, axis=0, keepdims=True)
        d_weights = dot_nt(values, upstream)
        d_scores = (weights.astype(F32) * (d_weights - delta) * factor).astype(BF16)
        grads[:size, columns(0)] = dot_nn(keys.T, d_scores).T.astype(BF16)
        grads[:size, columns(1)] = dot_nn(d_scores, queries).astype(BF16)
        grads[:size, columns(2)] = dot_nn(weights, upstream).astype(BF16)

    half = capacity // 2

    @pl.when(active & (live > half))
    def _():
        all_heads(capacity)

    @pl.when(active & (live <= half))
    def _():
        all_heads(half)

    @pl.when(active)
    def _():
        for copy in copies:
            copy.wait()
        step = min(512, 2 * block)

        def project(size):
            for first in range(0, 2 * block, step):
                product = dot_nt(grads[:size], w_vmem[first : first + step])
                partial[:size, first : first + step] = product.astype(BF16)
            if size < capacity:
                partial[size:] = jnp.zeros((capacity - size, 2 * block), BF16)
            for r in range(count):
                start = pl.multiple_of((me ^ r) * rows, rows)
                block_rows = partial[pl.ds(start, rows)]
                if grouped:
                    outs[r % 2][r // 2] = block_rows
                else:
                    outs[r][...] = block_rows

        @pl.when(live > half)
        def _():
            project(capacity)

        @pl.when(live <= half)
        def _():
            project(half)


def attend_call(info, saved, probs, mixed, d_attn, weight, other, count, grouped, section):
    capacity, width = d_attn.shape
    rows = capacity // count
    model_cols = 2 * weight.shape[1]
    heads = width // HEAD_DIM
    if grouped:
        outs, shape = 2, (count // 2, rows, model_cols)
    else:
        outs, shape = count, (rows, model_cols)
    once = pl.Buffered(1)
    return pl.pallas_call(
        functools.partial(attend_kernel, section),
        out_shape=[jax.ShapeDtypeStruct(shape, BF16)] * outs,
        grid_spec=pltpu.PrefetchScalarGridSpec(
            num_scalar_prefetch=1,
            grid=(1,),
            in_specs=[
                pl.BlockSpec((3, capacity, width), lambda h, info: (0, 0, 0), pipeline_mode=once),
                tail_spec(capacity),
                pl.BlockSpec((heads, capacity, capacity), lambda h, info: (0, 0, 0), pipeline_mode=once),
                pl.BlockSpec((capacity, width), lambda h, info: (0, 0), pipeline_mode=once),
                pl.BlockSpec((capacity, width), lambda h, info: (0, 0), pipeline_mode=once),
                pl.BlockSpec(memory_space=pl.ANY),
                pl.BlockSpec(memory_space=pl.ANY),
            ],
            out_specs=[pl.BlockSpec(shape, lambda h, info: (0,) * len(shape))] * outs,
            scratch_shapes=[
                pltpu.VMEM((capacity, 3 * width), BF16),
                pltpu.VMEM((capacity, model_cols), BF16),
                pltpu.VMEM((model_cols, 3 * width), BF16),
                pltpu.SemaphoreType.DMA((6,)),
            ],
        ),
        compiler_params=pltpu.CompilerParams(vmem_limit_bytes=20 * MIB),
        cost_estimate=SMALL,
        name="attend",
    )(info, saved, saved, probs, mixed, d_attn, weight, other)


def norm_kernel(pair, offsets, home, info, mods, tokens, d_output, upper, *rest):
    blocks, rest = rest[: len(offsets)], rest[len(offsets) :]
    d_norm = rest[-1]
    width = blocks[0].shape[1] // 2
    for offset, block in zip(offsets, blocks):
        owner = info[1] ^ offset
        for part in range(2):
            start = pl.multiple_of((owner ^ (part * pair)) * width, width)
            d_norm[:, pl.ds(start, width)] = block[:, part * width : (part + 1) * width].astype(F32)
    values = tokens[...].astype(F32)
    center = values - jnp.mean(values, axis=1, keepdims=True)
    inverse = lax.rsqrt(jnp.mean(center * center, axis=1, keepdims=True) + 1e-06)
    normed = center * inverse
    gained = d_norm[...] * (1.0 + mods[0:1])
    layer = inverse * (
        gained
        - jnp.mean(gained, axis=1, keepdims=True)
        - normed * jnp.mean(gained * normed, axis=1, keepdims=True)
    )
    d_input = (d_output[...].astype(F32) + layer).astype(BF16)
    if len(rest) == 2:
        rest[0][...] = jnp.where(info[2] == home, d_input, upper[...])
    else:
        next_mods, out, d_branch = rest[:3]
        out[...] = d_input
        gated = (next_mods[1:2] * d_input.astype(F32)).astype(BF16)
        d_branch[...] = jnp.where(info[2] == home, gated, upper[...])


def norm_call(info, pair, offsets, home, mods, tokens, d_output, upper, blocks, next_mods=()):
    rows, width = tokens.shape
    tile = 64
    block_width = blocks[0].shape[1]
    row_spec = lambda cols: pl.BlockSpec((tile, cols), lambda t, info: (t, 0))
    mods_spec = pl.BlockSpec(mods.shape, lambda t, info: (0, 0))
    outs = 1 + len(next_mods)
    return pl.pallas_call(
        functools.partial(norm_kernel, pair, offsets, home),
        out_shape=[jax.ShapeDtypeStruct((rows, width), BF16)] * outs,
        grid_spec=pltpu.PrefetchScalarGridSpec(
            num_scalar_prefetch=1,
            grid=(rows // tile,),
            in_specs=[mods_spec, row_spec(width), row_spec(width), row_spec(width)]
            + [row_spec(block_width)] * len(blocks)
            + [mods_spec] * len(next_mods),
            out_specs=[row_spec(width)] * outs,
            scratch_shapes=[pltpu.VMEM((tile, width), F32)],
        ),
        compiler_params=pltpu.CompilerParams(vmem_limit_bytes=20 * MIB),
        cost_estimate=SMALL,
        name="norm",
    )(info, mods, tokens, d_output, upper, *blocks, *next_mods)


def outer_kernel(sections, slots, count, info, *refs):
    out, joined = refs[-2], refs[-1]
    refs = iter(refs[:-2])
    rows = joined.shape[1] // count

    def chosen(options):
        value = options[0][...]
        for section in range(1, sections):
            value = jnp.where(info[2] == section, options[section][...], value)
        return value

    def take(amount):
        return [next(refs) for _ in range(amount)]

    total = None
    for slot in range(slots):
        mixed = take(1)[0][...] if slot == 0 else chosen(take(sections))
        for r in range(count):
            start = pl.multiple_of((info[0] ^ r) * rows, rows)
            single = r == 0 or slot > 0
            joined[slot, pl.ds(start, rows), :] = (
                take(1)[0][...] if single else chosen(take(sections))
            )
        term = dot_tn(mixed, joined[slot])
        total = term if total is None else total + term
    out[...] = total.astype(BF16)


def outer_call(part, pair, info, own_mixed, other_mixed, own_rows, other_rows, block_cols):
    capacity, width = own_mixed.shape
    count = len(own_rows)
    rows = capacity // count
    tile = block_cols
    per_block = block_cols // tile
    mixed_spec = pl.BlockSpec((capacity, width), lambda t, info: (0, 0))

    def own_map(t, info):
        return (0, (info[1] ^ (part * pair)) * per_block + t)

    def other_map(t, info):
        return (0, part * per_block + t)

    operands, specs = [own_mixed], [mixed_spec]
    for options in own_rows:
        operands += options
        specs += [pl.BlockSpec((rows, tile), own_map)] * len(options)
    for mixed, blocks in zip(other_mixed, other_rows):
        operands += mixed + blocks
        specs += [mixed_spec] * len(mixed) + [pl.BlockSpec((rows, tile), other_map)] * len(blocks)
    return pl.pallas_call(
        functools.partial(outer_kernel, len(own_rows[1]), 1 + len(other_mixed), count),
        out_shape=jax.ShapeDtypeStruct((width, block_cols), BF16),
        grid_spec=pltpu.PrefetchScalarGridSpec(
            num_scalar_prefetch=1,
            grid=(per_block,),
            in_specs=specs,
            out_specs=pl.BlockSpec((width, tile), lambda t, info: (0, t)),
            scratch_shapes=[pltpu.VMEM((1 + len(other_mixed), capacity, tile), BF16)],
        ),
        compiler_params=pltpu.CompilerParams(vmem_limit_bytes=24 * MIB),
        cost_estimate=SMALL,
        name="outer",
    )(info, *operands)


def after(value, *tokens):
    return lax.optimization_barrier((value, *tokens))[0]


def body(section_input, saved_qkv, modulation, w_qkv, w_out, lengths, student_out, teacher_target):
    section_total = lax.axis_size("section")
    seq_total = lax.axis_size("seq")
    dp_total = lax.axis_size("dp")
    section_pos = lax.axis_index("section")
    seq_pos = lax.axis_index("seq")
    dp_pos = lax.axis_index("dp")
    tokens = section_input[0, 0]
    mods = modulation[0, 0]
    shard_rows, model_width = tokens.shape
    capacity = saved_qkv.shape[2]
    block_cols = model_width // dp_total
    pair = 1
    offsets = [e for e in range(dp_total) if e & pair == 0]
    saved = saved_qkv[0, 0].transpose(1, 0, 2)
    weight = w_qkv[0].transpose(1, 0, 2)
    weight_out = w_out[0]

    def flat(section, seq, dp):
        return (section * seq_total + seq) * dp_total + dp

    def moved(value, sections, target):
        pairs = [
            (flat(s, i, j), flat(*target(s, i, j)))
            for s in sections
            for i in range(seq_total)
            for j in range(dp_total)
        ]
        return lax.ppermute(value, AXES, pairs)

    def over_dp(value, offset, sections, steps_down=0):
        return moved(value, sections, lambda s, i, j: (s - steps_down, i, j ^ offset))

    def over_seq(value, offset, sections):
        return moved(value, sections, lambda s, i, j: (s, i ^ offset, j))

    def section_shift(value, section, steps):
        return moved(value, [section], lambda s, i, j: (s + steps, i, j))

    info = jnp.stack([seq_pos, dp_pos, section_pos]).astype(jnp.int32)
    positions = seq_pos * shard_rows + jnp.arange(shard_rows, dtype=jnp.int32)
    gap = student_out[0].astype(F32) - teacher_target[0].astype(F32)
    loss_grad = jnp.where((positions < lengths[0])[:, None], gap, 0.0).astype(BF16)

    def prefetch(section, saved, weight):
        others = [over_dp(saved, e, [section]) for e in offsets[1:]]
        return others, over_dp(weight, pair, [section])

    def halved(kept, sent, sections, token):
        offset = 1
        while True:
            total = kept.astype(F32) + over_seq(sent, offset, sections).astype(F32)
            if total.shape[0] == 1:
                return total[0].astype(BF16)
            offset *= 2
            kept, sent = total[0::2], after(total[1::2].astype(BF16), token)

    def column_pair(rows, owner):
        first = lax.dynamic_slice_in_dim(rows, owner * block_cols, block_cols, 1)
        second = lax.dynamic_slice_in_dim(rows, (owner ^ 1) * block_cols, block_cols, 1)
        return jnp.concatenate([first, second], axis=1)

    def slots_of(saved_others):
        saved_slots = [saved_sent] + saved_others
        probs_slots = [own_probs] + [
            probs_call(info, saved_slots[k], capacity) for k in range(1, len(saved_slots))
        ]
        return saved_slots, probs_slots

    top = section_total - 1
    d_output = loss_grad
    d_branch = (mods[1] * d_output.astype(F32)).astype(BF16)
    high, low = lengths[0] // 256, lengths[0] % 256
    tail = jnp.zeros((3, TAIL, saved.shape[2]), BF16)
    tail = tail.at[0, 0, 0].set((high).astype(BF16))
    tail = tail.at[0, 0, 1].set((low).astype(BF16))
    saved_sent = jnp.concatenate([saved, tail], axis=1)
    prefetched = prefetch(top, saved_sent, weight)
    own_probs = probs_call(info, saved_sent, capacity)
    grad_up, uppers = None, []
    held = (own_probs[1],)
    every = list(range(section_total))
    rows_of, mixed_of = [None] * section_total, [None] * section_total
    for section in reversed(every):
        only = [section]
        saved_others, weight_other = prefetched
        own_rows = [d_branch] + [over_seq(d_branch, r, only) for r in range(1, seq_total)]
        if section < top:
            saved_slots, probs_slots = slots_of(saved_others)
            held = held + (probs_slots[-1][1],)
        ready_rows = own_rows[:-1] + [after(own_rows[-1], *held)] if held else own_rows
        d_attn = d_attn_call(info, ready_rows, weight_out)
        if section == top:
            saved_slots, probs_slots = slots_of(saved_others)
        leaving = d_attn
        if section == 0:
            all_columns = [
                over_dp(column_pair(d_branch, dp_pos ^ e), e, every) for e in offsets[1:]
            ]
        d_attns = [d_attn] + [over_dp(leaving, e, only) for e in offsets[1:]]
        rows_of[section] = own_rows
        mixed_of[section] = [mixed for _, mixed in probs_slots[1:]]

        waits = ()
        all_parts = {}
        for k in range(len(offsets)):
            probs, mixed = probs_slots[k]
            if k == 1 and section > 0:
                ready = [mixed for _, mixed in probs_slots[1:]]
                next_mods = section_shift(after(mods, *waits, *ready, *d_attns[1:]), section, -1)
                next_saved = [
                    over_dp(after(saved_sent, next_mods), e, [section - 1]) for e in offsets[1:]
                ]
                waits = waits + (next_mods,)
            all_parts[k] = attend_call(
                info,
                saved_slots[k],
                probs,
                mixed,
                after(d_attns[k], *waits) if waits else d_attns[k],
                weight,
                weight_other,
                seq_total,
                k == 0,
                section,
            )
            waits = (all_parts[k][0],)
        if section > 0:
            next_other = over_dp(after(weight, *waits), pair, [section - 1])
            next_tokens = section_shift(after(tokens, probs_slots[-1][1]), section, -1)
        down = 1 if section > 0 else 0
        home = [None] * len(offsets)
        for k in reversed(range(len(offsets))):
            parts = all_parts[k]
            if k == 0:
                ready = [mixed for _, mixed in probs_slots[1:]] + d_attns[1:]
                late = waits[0] if section == top else total
                total = halved(parts[0], after(parts[1], *ready), only, late)
            else:
                total = parts[0].astype(F32)
                for r in range(1, seq_total):
                    total = total + over_seq(parts[r], r, only).astype(F32)
                total = total.astype(BF16)
            e = offsets[k]
            home[k] = over_dp(total, e, only, down) if e or down else total

        if section > 0:
            prefetched = next_saved, next_other
            d_output, d_branch = norm_call(
                info,
                pair,
                offsets,
                section - 1,
                next_mods,
                next_tokens,
                d_output,
                d_branch,
                home,
                (mods,),
            )
            uppers.append((section, d_output))
            held = ()
    for section, d_input in uppers:
        back = section_shift(after(d_input, *waits), section - 1, 1)
        grad_up = back if grad_up is None else jnp.where(section_pos == section, back, grad_up)
    (grad_in,) = norm_call(info, pair, offsets, 0, mods, tokens, d_output, grad_up, home)

    other_rows = [
        [columns] + [over_seq(columns, r, every) for r in range(1, seq_total)]
        for columns in all_columns
    ]
    row_options = [[rows_of[s][r] for s in every] for r in range(1, seq_total)]
    mixed_options = [[mixed_of[s][k] for s in every] for k in range(len(offsets) - 1)]

    def outer_part(part, *tokens):
        own_options = [[after(d_branch, *tokens)]] + row_options
        return outer_call(
            part, pair, info, own_probs[1], mixed_options, own_options, other_rows, block_cols
        )

    received = over_dp(outer_part(1, *waits), pair, every)
    kept = outer_part(0, received)
    grad_out = (kept.astype(F32) + received.astype(F32)).astype(BF16)
    return grad_in[None, None], grad_out[None]


def solution(mesh):
    in_specs = (
        P("section", "dp", "seq", None),
        P("section", "dp", None, None, "seq"),
        P("section", "dp", None, None),
        P("section", "dp", None, "seq"),
        P("section", "seq", None),
        P("dp"),
        P("dp", "seq", None),
        P("dp", "seq", None),
    )
    out_specs = (P("section", "dp", "seq", None), P("section", "seq", "dp"))
    return jax.shard_map(body, mesh=mesh, in_specs=in_specs, out_specs=out_specs, check_vma=False)
```
